128 devices in a mesh: seq: 8 (over z, core), grp: 16 (over x, y).
Axes of the slice: x: 4, y: 4, z: 4, core: 2. Of those that a mesh axis runs over, the one named last changes fastest.
Arguments:
- mamba_input: bfloat16 [16, 1024, 8192], P('grp', 'seq'), may hold values from -6 to 6
- gate_input: bfloat16 [16, 1024, 8192], P('grp', 'seq'), may hold values from -6 to 6
- step_raw: bfloat16 [16, 1024, 8192], P('grp', 'seq'), may hold values from -12 to 8
- scan_proj: bfloat16 [16, 2, 16, 1024], P('grp', None, None, 'seq'), may hold values from -3 to 3
- decay_log: float32 [16, 8192], replicated, may hold values from -4 to 7
- step_bias: float32 [8192], replicated, may hold values from -0.5 to 0.5
- conv_weight: float32 [4, 8192], replicated, may hold values from -3 to 3
- conv_bias: float32 [8192], replicated, may hold values from -0.5 to 0.5
- skip_gain: float32 [8192], replicated, may hold values from 0.5 to 1.5
- kv_rows: bfloat16 [16, 1024, 2048], P('grp', 'seq'), may hold values from -6 to 6
- decode_device: int32 [16], replicated, may hold values from 0 to 15, as said below
- block_count: int32 [16], replicated, may hold values from 1 to 64, as said below
- block_slot: int32 [16, 64], replicated, may hold values from 0 to 23, as said below
Outputs:
- block_out: bfloat16 [16, 1024, 8192], P('grp', 'seq')
- kv_cache: bfloat16 [16, 8, 24, 16, 2048], P('grp', 'seq')
- ssm_cache: float32 [16, 3, 16, 8192], P('grp', None, None, 'seq')
- conv_cache: bfloat16 [16, 3, 3, 8192], P('grp', None, None, 'seq')
The draws below stay inside these ranges and needn't reach their ends.
Inputs may be any that keep to these rules, and one draw needn't show every extreme that they name: `decode_device`: no decode device takes more than 3 requests, and some decode device takes exactly 3. `block_count`: some request has all 64 blocks. `block_slot`: blocks b < block_count of requests with the same decode device and the same b // 8 have distinct slots.
All inputs are finite; a program needn't handle non-finite values.
Results may differ from the reference program's by a relative error of at most 0.013.
Values may be sent and summed in bfloat16 or wider, within the bound.
No kernel may reach another device: no remote copies, remote signals or barrier semaphores. Data moves between devices by JAX's collectives and lax.ppermute only.
A program may use at most 192 MiB of HBM per device.

```python
import math
import jax
import jax.numpy as jnp
from jax import lax

INNER_FEATURES = 8192
NSTATE = 16
KCONV = 4
KVW = 2048
BLOCK = 16
MOST = 3
SPURT_SPAN = 4
QUERY_SPAN = 1024
QUERY_TOTAL = 16
SB = 8
NBLK = 64
CAP = 24
N_SEQ = 8
N_GRP = 16


def destination_list(key):
    base_key = jax.random.fold_in(key, 11)
    first_key, random_seed_middle, random_seed_latter = jax.random.split(base_key, 3)
    crowded = jax.random.randint(first_key, (), 0, QUERY_TOTAL)
    spares = (crowded + 1 + jnp.arange((QUERY_TOTAL - 1) * MOST) // MOST) % QUERY_TOTAL
    spares = jax.random.permutation(random_seed_middle, spares)[:QUERY_TOTAL - MOST]
    assigned = jnp.concatenate([jnp.full((MOST,), crowded), spares])
    return jax.random.permutation(random_seed_latter, assigned).astype(jnp.int32)


def draw_decode_device(key, part):
    return destination_list(key)


def draw_block_slot(key, part):
    assigned = destination_list(key)
    key = jax.random.fold_in(key, 2)
    same_dest = assigned[:, None] == assigned[None, :]
    earlier = jnp.arange(QUERY_TOTAL)[None, :] < jnp.arange(QUERY_TOTAL)[:, None]
    ranking = jnp.sum((same_dest & earlier).astype(jnp.int32), axis=1)
    segments = NBLK // SB
    offset = jax.random.randint(key, (QUERY_TOTAL, segments), 0, CAP)
    block_index = jnp.arange(NBLK)
    shift_rows = offset[assigned][:, block_index // SB]
    slots = (ranking[:, None] * SB + (block_index % SB)[None, :] + shift_rows) % CAP
    return slots.astype(jnp.int32)


def draw_block_count(key, part):
    key = jax.random.fold_in(key, 3)
    first_key, random_seed_middle = jax.random.split(key)
    counts = jax.random.randint(first_key, (QUERY_TOTAL,), 1, NBLK + 1)
    longest = jax.random.randint(random_seed_middle, (), 0, QUERY_TOTAL)
    counts = jnp.where(jnp.arange(QUERY_TOTAL) == longest, NBLK, counts)
    return counts.astype(jnp.int32)


def draw_decay_log(key, part):
    key = jax.random.fold_in(key, 4)
    first_key, random_seed_middle, random_seed_latter = jax.random.split(key, 3)
    slow_share = 0.5
    is_slow = jax.random.bernoulli(first_key, slow_share, (1, INNER_FEATURES))
    slow_rate = jnp.exp(jax.random.uniform(random_seed_middle, (NSTATE, INNER_FEATURES), jnp.float32, math.log(0.04), math.log(0.1)))
    fast_rate = jnp.exp(jax.random.uniform(random_seed_latter, (NSTATE, INNER_FEATURES), jnp.float32, math.log(0.5), math.log(2.0))) * (QUERY_SPAN / 80.0)
    return jnp.log(jnp.where(is_slow, slow_rate, fast_rate)).astype(jnp.float32)


def draw_step_raw(key, part):
    key = jax.random.fold_in(key, 5)
    first_key, random_seed_middle, random_seed_latter = jax.random.split(key, 3)
    factor = jnp.exp(jax.random.uniform(first_key, (QUERY_TOTAL, QUERY_SPAN, INNER_FEATURES), jnp.float32, math.log(0.5), math.log(2.0)))
    drawn_matrix = jnp.log(jnp.expm1(factor * (2.0 / QUERY_SPAN)))
    spurt_matrix = jax.random.randint(random_seed_middle, (QUERY_TOTAL, SPURT_SPAN), 0, QUERY_SPAN)
    spurt_index = jnp.any(jnp.arange(QUERY_SPAN)[None, :, None] == spurt_matrix[:, None, :], axis=-1)
    spurt_entry = jax.random.uniform(random_seed_latter, (QUERY_TOTAL, QUERY_SPAN, INNER_FEATURES), jnp.float32, 3.0, 8.0)
    return jnp.where(spurt_index[:, :, None], spurt_entry, drawn_matrix).astype(jnp.bfloat16)


def shard_levels(own_key, shape, shards, least, high):
    level, own = 1.0, jax.random.fold_in(own_key, 6)
    for dim, blocks in shards:
        heights = jnp.exp(jax.random.uniform(jax.random.fold_in(own, dim), (blocks,), jnp.float32, least / len(shards), high / len(shards)))
        level = level * jnp.repeat(heights, shape[dim] // blocks).reshape([-1 if axis == dim else 1 for axis in range(len(shape))])
    return level


def centred(own_key, shape, width, bound, shards=(), kind=jnp.bfloat16):
    loudness = shard_levels(own_key, shape, shards, -0.22, 0.18) if shards else 1.0
    result = jax.random.normal(own_key, shape, jnp.float32) * width * loudness
    return jnp.minimum(jnp.maximum(result, -bound), bound).astype(kind)


def setup_inputs(seed: int = 0) -> dict:
    splits = jax.random.split(jax.random.key(seed), 14)
    return {
        "mamba_input": centred(splits[0], (QUERY_TOTAL, QUERY_SPAN, INNER_FEATURES), 1.0, 6.0, ((0, 16), (1, 8))),
        "gate_input": centred(splits[1], (QUERY_TOTAL, QUERY_SPAN, INNER_FEATURES), 1.0, 6.0, ((0, 16), (1, 8))),
        "step_raw": draw_step_raw(jax.random.fold_in(splits[13], 71), 0),
        "scan_proj": centred(splits[3], (QUERY_TOTAL, 2, NSTATE, QUERY_SPAN), 0.5, 3.0, ((0, 16), (3, 8))),
        "decay_log": draw_decay_log(jax.random.fold_in(splits[13], 71), 0),
        "step_bias": jnp.clip(jax.random.uniform(splits[5], (INNER_FEATURES,), jnp.float32, -0.5, 0.5), -0.5, 0.5),
        "conv_weight": centred(splits[6], (KCONV, INNER_FEATURES), KCONV ** -0.5, 3.0, (), jnp.float32),
        "conv_bias": jnp.clip(jax.random.uniform(splits[7], (INNER_FEATURES,), jnp.float32, -0.5, 0.5), -0.5, 0.5),
        "skip_gain": jnp.clip(jax.random.uniform(splits[8], (INNER_FEATURES,), jnp.float32, 0.5, 1.5), 0.5, 1.5),
        "kv_rows": centred(splits[9], (QUERY_TOTAL, QUERY_SPAN, KVW), 1.0, 6.0, ((0, 16), (1, 8))),
        "decode_device": draw_decode_device(jax.random.fold_in(splits[13], 71), 0),
        "block_count": draw_block_count(jax.random.fold_in(splits[13], 71), 0),
        "block_slot": draw_block_slot(jax.random.fold_in(splits[13], 71), 0),
    }


inner_len = 16


def chain_scan(start_carry, step_size, driven, b_rows, c_rows, decay_rates):
    length = step_size.shape[0]
    blocks = length // inner_len
    step_blk = step_size.reshape(blocks, inner_len, -1)
    drive_blk = (step_size * driven).reshape(blocks, inner_len, -1)
    b_blk = b_rows.reshape(b_rows.shape[0], blocks, inner_len).transpose(1, 2, 0)
    c_blk = c_rows.reshape(c_rows.shape[0], blocks, inner_len).transpose(1, 2, 0)

    def advance(carry, blk_data):
        step_now, drive_now, b_now, c_now = blk_data
        decay_now = jnp.exp(step_now[:, None, :] * decay_rates[None])
        values = []
        for t in range(inner_len):
            carry = decay_now[t] * carry + drive_now[t][None, :] * b_now[t][:, None]
            values.append(jnp.sum(c_now[t][:, None] * carry, axis=0))
        return carry, jnp.stack(values)

    final_carry, outputs = lax.scan(advance, start_carry, (step_blk, drive_blk, b_blk, c_blk))
    return final_carry, outputs.reshape(length, -1)


def convolve(padded, conv_weight, conv_bias, length):
    summed = conv_bias[None, :] + jnp.zeros((length, padded.shape[1]), jnp.float32)
    for k in range(KCONV):
        summed = summed + conv_weight[k][None, :] * padded[k:k + length]
    return jax.nn.silu(summed)


def request_rank(decode_device):
    requests = decode_device.shape[0]
    same_dest = decode_device[:, None] == decode_device[None, :]
    earlier = jnp.arange(requests)[None, :] < jnp.arange(requests)[:, None]
    return jnp.sum((same_dest & earlier).astype(jnp.int32), axis=1)


def reference(mamba_input, gate_input, step_raw, scan_proj, decay_log, step_bias, conv_weight, conv_bias, skip_gain, kv_rows, decode_device, block_count, block_slot):
    decay_rates = -jnp.exp(decay_log)
    places = jnp.arange(QUERY_SPAN)
    is_live = places[None, :] < (block_count * BLOCK)[:, None]
    padded = jnp.concatenate([jnp.zeros((QUERY_TOTAL, KCONV - 1, INNER_FEATURES), jnp.float32), mamba_input.astype(jnp.float32)], axis=1)

    def one_prompt(padded_one, gate_one, raw_one, proj_one, live_one):
        driven = convolve(padded_one, conv_weight, conv_bias, QUERY_SPAN)
        step_size = jax.nn.softplus(raw_one.astype(jnp.float32) + step_bias[None, :]) * live_one[:, None].astype(jnp.float32)
        zero_state = jnp.zeros((NSTATE, INNER_FEATURES), jnp.float32)
        final_carry, scanned = chain_scan(zero_state, step_size, driven, proj_one[0].astype(jnp.float32), proj_one[1].astype(jnp.float32), decay_rates)
        mixed_rows = (scanned + skip_gain[None, :] * driven) * jax.nn.silu(gate_one.astype(jnp.float32))
        mixed_rows = jnp.where(live_one[:, None], mixed_rows, 0.0).astype(jnp.bfloat16)
        return mixed_rows, final_carry

    block_out, finals = jax.vmap(one_prompt)(padded, gate_input, step_raw, scan_proj, is_live)

    ranking = request_rank(decode_device)
    where_state = (decode_device * MOST + ranking).astype(jnp.int32)
    ssm_cache = jnp.zeros((N_GRP * MOST, NSTATE, INNER_FEATURES), jnp.float32).at[where_state].set(finals).reshape(N_GRP, MOST, NSTATE, INNER_FEATURES)

    def last_rows(rows_one, count_one):
        return lax.dynamic_slice_in_dim(rows_one, (count_one * BLOCK - (KCONV - 1)).astype(jnp.int32), KCONV - 1, 0)

    tails = jax.vmap(last_rows)(mamba_input, block_count)
    conv_cache = jnp.zeros((N_GRP * MOST, KCONV - 1, INNER_FEATURES), jnp.bfloat16).at[where_state].set(tails).reshape(N_GRP, MOST, KCONV - 1, INNER_FEATURES)

    blocks = kv_rows.reshape(QUERY_TOTAL, NBLK, BLOCK, KVW)
    block_index = jnp.arange(NBLK).astype(jnp.int32)
    target = (decode_device[:, None] * N_SEQ + (block_index // SB)[None, :]) * CAP + block_slot
    is_valid = block_index[None, :] < block_count[:, None]
    spare = N_GRP * N_SEQ * CAP
    target = jnp.where(is_valid, target, spare).reshape(-1).astype(jnp.int32)
    kv_cache = jnp.zeros((spare + 1, BLOCK, KVW), jnp.bfloat16).at[target].set(blocks.reshape(-1, BLOCK, KVW))[:spare]
    kv_cache = kv_cache.reshape(N_GRP, N_SEQ, CAP, BLOCK, KVW)
    return block_out, kv_cache, ssm_cache, conv_cache
```

```python
import functools

import jax
import jax.numpy as jnp
from jax import lax
from jax.experimental import pallas as pl
from jax.experimental.pallas import tpu as pltpu
from jax.sharding import PartitionSpec as P

NSTATE = 16
KCONV = 4
BLOCK = 16
MOST = 3
LANES = 128
LOG2E = 1.4426950408889634
MSG = 32
VMEM_BYTES = 48 * 1024 * 1024
F32 = jnp.float32
BF16 = jnp.bfloat16

VM = functools.partial(pl.BlockSpec, memory_space=pltpu.VMEM)
SM = pl.BlockSpec(memory_space=pltpu.SMEM)


def silu(v):
    return v * (1.0 / (1.0 + jnp.exp(-v)))


def softplus(v):
    return jnp.maximum(v, 0.0) + jnp.log1p(jnp.exp(-jnp.abs(v)))


def split(v):
    high = v.astype(BF16)
    return high, (v - high.astype(F32)).astype(BF16)


def scan_kernel(
    width,
    place_ref,
    x_ref,
    halo_ref,
    step_ref,
    log_ref,
    sbias_ref,
    cw_ref,
    cbias_ref,
    skip_ref,
    b_ref,
    c_ref,
    out_ref,
    run_ref,
    msg_ref,
    pad_s,
    dt_s,
    drive_s,
    mix_s,
):
    length, channels = x_ref.shape
    groups = length // NSTATE
    seg_end = place_ref[0]
    live = lax.broadcasted_iota(jnp.int32, (length, width), 0) < seg_end
    row = lax.broadcasted_iota(jnp.int32, (length, length), 0)
    col = lax.broadcasted_iota(jnp.int32, (length, length), 1)
    tri = (col <= row).astype(BF16)
    held = jnp.logical_and(seg_end >= 1, seg_end <= length)
    held = jnp.logical_and(held, place_ref[1] > 0)
    tail_at = pl.multiple_of(jnp.clip(seg_end, 8, length), 8)

    for lane in range(0, channels, width):
        cut = pl.ds(lane, width)
        pad_s[pl.ds(0, 8), :] = jnp.concatenate(
            [jnp.zeros((8 - (KCONV - 1), width), F32), halo_ref[:, cut].astype(F32)], axis=0
        )
        pad_s[pl.ds(8, length), :] = x_ref[:, cut].astype(F32)
        summed = jnp.broadcast_to(cbias_ref[:, cut], (length, width))
        for k in range(KCONV):
            summed = summed + cw_ref[pl.ds(k, 1), cut] * pad_s[pl.ds(8 - (KCONV - 1) + k, length), :]
        driven = silu(summed)
        raw = step_ref[:, cut].astype(F32) + sbias_ref[:, cut]
        dt = jnp.where(live, softplus(raw), 0.0)
        dt_s[...] = dt.reshape(groups, NSTATE, width)
        drive_s[...] = (dt * driven).reshape(groups, NSTATE, width)
        high, low = split(dt)
        run = jnp.dot(tri, high, preferred_element_type=F32) + jnp.dot(
            tri, low, preferred_element_type=F32
        )
        run_ref[:, cut] = run
        out_ref[:, cut] = skip_ref[:, cut] * driven
        rates = -LOG2E * jnp.exp(log_ref[:, cut])

        def one_group(i, state):
            for tt in range(NSTATE):
                dt_now = dt_s[i, pl.ds(tt, 1), :]
                drive_now = drive_s[i, pl.ds(tt, 1), :]
                b_now = jnp.concatenate([b_ref[i * NSTATE + tt]] * (width // LANES), axis=1)
                state = jnp.exp2(dt_now * rates) * state + drive_now * b_now
                mix_s[pl.ds(tt * NSTATE, NSTATE), :] = state.astype(BF16)
            rows = pl.ds(pl.multiple_of(i * NSTATE, NSTATE), NSTATE)
            out_ref[rows, cut] += jnp.dot(c_ref[i], mix_s[...], preferred_element_type=F32)
            return state

        state = lax.fori_loop(0, groups, one_group, jnp.zeros((NSTATE, width), F32))
        msg_ref[0, pl.ds(0, NSTATE), cut] = state.astype(BF16)
        s_high, s_low = split(run[length - 1 :, :])
        tail = pad_s[pl.ds(tail_at, 8), :] * held.astype(F32)
        extra = jnp.concatenate(
            [
                s_high.astype(F32),
                s_low.astype(F32),
                tail[8 - (KCONV - 1) :],
                jnp.zeros((MSG - NSTATE - 2 - (KCONV - 1), width), F32),
            ],
            axis=0,
        )
        msg_ref[0, pl.ds(NSTATE, MSG - NSTATE), cut] = extra.astype(BF16)


def local_scan(place, x, halo, step, log, sbias, cw, cbias, skip, b_wide, c_diag, pieces, width=512):
    length, channels = x.shape
    piece = channels // pieces
    per = lambda rows: pl.BlockSpec((rows, piece), lambda j: (0, j))
    whole = lambda a: pl.BlockSpec(a.shape, lambda j: (0,) * a.ndim)
    return pl.pallas_call(
        functools.partial(scan_kernel, width),
        grid=(pieces,),
        in_specs=[
            SM,
            per(length),
            per(halo.shape[0]),
            per(length),
            per(NSTATE),
            per(1),
            per(KCONV),
            per(1),
            per(1),
            whole(b_wide),
            whole(c_diag),
        ],
        out_specs=[
            per(length),
            per(length),
            pl.BlockSpec((1, MSG, piece), lambda j: (j, 0, 0)),
        ],
        out_shape=[
            jax.ShapeDtypeStruct((length, channels), F32),
            jax.ShapeDtypeStruct((length, channels), F32),
            jax.ShapeDtypeStruct((pieces, MSG, piece), BF16),
        ],
        scratch_shapes=[
            pltpu.VMEM((length + 8, width), F32),
            pltpu.VMEM((length // NSTATE, NSTATE, width), F32),
            pltpu.VMEM((length // NSTATE, NSTATE, width), F32),
            pltpu.VMEM((NSTATE * NSTATE, width), BF16),
        ],
        compiler_params=pltpu.CompilerParams(vmem_limit_bytes=VMEM_BYTES),
        cost_estimate=pl.CostEstimate(
            flops=8 * length * channels * NSTATE,
            bytes_accessed=16 * length * channels,
            transcendentals=length * channels * NSTATE,
        ),
        name="local_scan",
    )(place, x, halo, step, log, sbias, cw, cbias, skip, b_wide, c_diag)


def chain_kernel(place_ref, got_ref, log_ref, start_ref, final_ref):
    pieces, _, piece = got_ref.shape
    rates = -LOG2E * jnp.exp(log_ref[...])
    state = jnp.zeros((NSTATE, piece), F32)
    tails = jnp.zeros((NSTATE, piece), F32)
    for r in range(pieces):
        start_ref[r] = state.astype(BF16)
        extra = got_ref[r, pl.ds(NSTATE, MSG - NSTATE), :].astype(F32)
        total = extra[0:1] + extra[1:2]
        state = jnp.exp2(total * rates) * state + got_ref[r, pl.ds(0, NSTATE), :].astype(F32)
        tails = tails + extra
    final_ref[...] = jnp.zeros_like(final_ref)
    dest = place_ref[2]
    final_ref[dest, pl.ds(0, NSTATE), :] = state.astype(BF16)
    final_ref[dest, pl.ds(NSTATE, MSG - NSTATE), :] = tails.astype(BF16)


def chain(place, got, log_piece, groups):
    pieces, _, piece = got.shape
    return pl.pallas_call(
        chain_kernel,
        in_specs=[SM, VM(), VM()],
        out_specs=[VM(), VM()],
        out_shape=[
            jax.ShapeDtypeStruct((pieces, NSTATE, piece), BF16),
            jax.ShapeDtypeStruct((groups, MSG, piece), BF16),
        ],
        compiler_params=pltpu.CompilerParams(vmem_limit_bytes=VMEM_BYTES),
        name="chain",
    )(place, got, log_piece)


def finish_kernel(
    width, place_ref, start_ref, out_ref, run_ref, log_ref, gate_ref, c_ref, mixed_ref, run_s, mix_s
):
    length, channels = gate_ref.shape
    groups = length // NSTATE
    seg_end = place_ref[0]
    for lane in range(0, channels, width):
        cut = pl.ds(lane, width)
        run_s[...] = run_ref[:, cut].reshape(groups, NSTATE, width)
        rates = -LOG2E * jnp.exp(log_ref[:, cut])
        start = start_ref[0, :, cut]

        def one_group(i, carry):
            for tt in range(NSTATE):
                power = (run_s[i, pl.ds(tt, 1), :] * rates).astype(BF16)
                mix_s[pl.ds(tt * NSTATE, NSTATE), :] = jnp.exp2(power) * start
            rows = pl.ds(pl.multiple_of(i * NSTATE, NSTATE), NSTATE)
            carried = jnp.dot(c_ref[i], mix_s[...], preferred_element_type=F32)
            mixed = (out_ref[rows, cut] + carried) * silu(gate_ref[rows, cut].astype(F32))
            at = lax.broadcasted_iota(jnp.int32, (NSTATE, width), 0) + i * NSTATE
            mixed_ref[rows, cut] = jnp.where(at < seg_end, mixed, 0.0).astype(BF16)
            return carry

        lax.fori_loop(0, groups, one_group, 0)


def finish(place, start, out, run, log, gate, c_diag, width=512):
    length, channels = gate.shape
    pieces, _, piece = start.shape
    per = lambda rows: pl.BlockSpec((rows, piece), lambda j: (0, j))
    return pl.pallas_call(
        functools.partial(finish_kernel, width),
        grid=(pieces,),
        in_specs=[
            SM,
            pl.BlockSpec((1, NSTATE, piece), lambda j: (j, 0, 0)),
            per(length),
            per(length),
            per(NSTATE),
            per(length),
            pl.BlockSpec(c_diag.shape, lambda j: (0, 0, 0)),
        ],
        out_specs=per(length),
        out_shape=jax.ShapeDtypeStruct((length, channels), BF16),
        scratch_shapes=[
            pltpu.VMEM((length // NSTATE, NSTATE, width), F32),
            pltpu.VMEM((NSTATE * NSTATE, width), BF16),
        ],
        compiler_params=pltpu.CompilerParams(vmem_limit_bytes=VMEM_BYTES),
        cost_estimate=pl.CostEstimate(
            flops=4 * length * channels * NSTATE,
            bytes_accessed=12 * length * channels,
            transcendentals=length * channels * NSTATE // 2,
        ),
        name="finish",
    )(place, start, out, run, log, gate, c_diag)


def caches_kernel(place_ref, dest_ref, got_ref, state_ref, rows_ref):
    groups = got_ref.shape[0]
    grp_pos = place_ref[3]
    state_ref[...] = jnp.zeros_like(state_ref)
    rows_ref[...] = jnp.zeros_like(rows_ref)

    def one(g, taken):
        mine = dest_ref[g] == grp_pos

        @pl.when(mine)
        def _():
            state_ref[taken] = got_ref[g, pl.ds(0, NSTATE), :].astype(F32)
            extra = got_ref[g, pl.ds(NSTATE, MSG - NSTATE), :]
            rows_ref[taken] = extra[2 : 2 + KCONV - 1]

        return taken + mine.astype(jnp.int32)

    lax.fori_loop(0, groups, one, jnp.int32(0))


def caches(place, decode_device, got):
    piece = got.shape[2]
    return pl.pallas_call(
        caches_kernel,
        in_specs=[SM, SM, VM()],
        out_specs=[VM(), VM()],
        out_shape=[
            jax.ShapeDtypeStruct((MOST, NSTATE, piece), F32),
            jax.ShapeDtypeStruct((MOST, KCONV - 1, piece), BF16),
        ],
        compiler_params=pltpu.CompilerParams(vmem_limit_bytes=VMEM_BYTES),
        name="caches",
    )(place, decode_device, got)


def kv_kernel(here, place_ref, dest_ref, count_ref, slot_ref, rows_ref, cache_ref, zero_s, used_s, sems):
    groups, capacity = rows_ref.shape[0], cache_ref.shape[0]
    grp_pos, first = place_ref[3], place_ref[4]
    zero_s[...] = jnp.zeros_like(zero_s)

    def clear(c, carry):
        used_s[c] = 0
        return carry

    lax.fori_loop(0, capacity, clear, 0)

    def request(g, carry):
        @pl.when(dest_ref[g] == grp_pos)
        def _():
            def block(j, carry):
                slot = slot_ref[g, first + j]
                used_s[slot] = 1
                pltpu.make_async_copy(rows_ref.at[g, j], cache_ref.at[slot], sems.at[slot]).start()
                return carry

            lax.fori_loop(0, jnp.clip(count_ref[g] - first, 0, here), block, 0)

        return carry

    lax.fori_loop(0, groups, request, 0)

    def fill(c, carry):
        @pl.when(used_s[c] == 0)
        def _():
            pltpu.make_async_copy(zero_s, cache_ref.at[c], sems.at[c]).start()

        return carry

    lax.fori_loop(0, capacity, fill, 0)

    def finish_copy(c, carry):
        pltpu.make_async_copy(zero_s, cache_ref.at[c], sems.at[c]).wait()
        return carry

    lax.fori_loop(0, capacity, finish_copy, 0)


def place_kv(place, decode_device, block_count, block_slot, rows, here, capacity):
    width = rows.shape[-1]
    return pl.pallas_call(
        functools.partial(kv_kernel, here),
        in_specs=[SM, SM, SM, SM, pl.BlockSpec(memory_space=pl.ANY)],
        out_specs=pl.BlockSpec(memory_space=pl.ANY),
        out_shape=jax.ShapeDtypeStruct((capacity, BLOCK, width), BF16),
        scratch_shapes=[
            pltpu.VMEM((BLOCK, width), BF16),
            pltpu.SMEM((capacity,), jnp.int32),
            pltpu.SemaphoreType.DMA((capacity,)),
        ],
        name="place_kv",
    )(place, decode_device, block_count, block_slot, rows)


def per_device(
    mamba_input,
    gate_input,
    step_raw,
    scan_proj,
    decay_log,
    step_bias,
    conv_weight,
    conv_bias,
    skip_gain,
    kv_rows,
    decode_device,
    block_count,
    block_slot,
):
    seg_len, channels = mamba_input.shape[1:]
    groups = lax.axis_size("grp")
    pieces = lax.axis_size("seq")
    piece = channels // pieces
    seq_pos = lax.axis_index("seq")
    grp_pos = lax.axis_index("grp")
    here = seg_len // BLOCK
    capacity = MOST * here
    x = mamba_input[0]

    kv_all = lax.all_gather(kv_rows[0].reshape(here, BLOCK, kv_rows.shape[2]), "grp")
    halo = lax.ppermute(
        x[seg_len - (KCONV - 1) :], "seq", [(s, s + 1) for s in range(pieces - 1)]
    )
    own_count = block_count[grp_pos]
    place = jnp.stack(
        [
            own_count * BLOCK - seq_pos * seg_len,
            jnp.int32(1),
            decode_device[grp_pos],
            grp_pos,
            seq_pos * here,
        ]
    ).astype(jnp.int32)
    b_wide = jnp.broadcast_to(
        scan_proj[0, 0].T.astype(F32)[:, :, None], (seg_len, NSTATE, LANES)
    )
    c_blk = scan_proj[0, 1].T.reshape(seg_len // NSTATE, NSTATE, NSTATE)
    c_diag = (c_blk[:, :, None, :] * jnp.eye(NSTATE, dtype=BF16)[None, :, :, None]).reshape(
        seg_len // NSTATE, NSTATE, NSTATE * NSTATE
    )

    out, run, msg = local_scan(
        place,
        x,
        halo,
        step_raw[0],
        decay_log,
        step_bias[None],
        conv_weight,
        conv_bias[None],
        skip_gain[None],
        b_wide,
        c_diag,
        pieces,
    )
    got = lax.all_to_all(msg, "seq", split_axis=0, concat_axis=0, tiled=True)
    log_piece = lax.dynamic_slice_in_dim(decay_log, seq_pos * piece, piece, 1)
    starts, final = chain(place, got, log_piece, groups)
    start = lax.all_to_all(starts, "seq", split_axis=0, concat_axis=0, tiled=True)
    final_got = lax.all_to_all(final, "grp", split_axis=0, concat_axis=0, tiled=True)
    block_out = finish(place, start, out, run, decay_log, gate_input[0], c_diag)
    ssm_cache, conv_cache = caches(place, decode_device, final_got)
    kv_cache = place_kv(place, decode_device, block_count, block_slot, kv_all, here, capacity)
    return block_out[None], kv_cache[None, None], ssm_cache[None], conv_cache[None]


def solution(mesh):
    return jax.shard_map(
        per_device,
        mesh=mesh,
        in_specs=(
            P("grp", "seq", None),
            P("grp", "seq", None),
            P("grp", "seq", None),
            P("grp", None, None, "seq"),
            P(),
            P(),
            P(),
            P(),
            P(),
            P("grp", "seq", None),
            P(),
            P(),
            P(),
        ),
        out_specs=(
            P("grp", "seq", None),
            P("grp", "seq", None, None, None),
            P("grp", None, None, "seq"),
            P("grp", None, None, "seq"),
        ),
        check_vma=False,
    )
```

```python
import functools

import jax
import jax.numpy as jnp
import numpy as np
from jax import lax
from jax.experimental import pallas as pl
from jax.experimental.pallas import tpu as pltpu
from jax.sharding import PartitionSpec as P

NSTATE = 16
KCONV = 4
BLOCK = 16
MOST = 3
LANES = 128
RIM = 8
LOG2E = 1.4426950408889634
MSG = 32
VMEM_BYTES = 48 * 1024 * 1024
F32 = jnp.float32
BF16 = jnp.bfloat16

VM = functools.partial(pl.BlockSpec, memory_space=pltpu.VMEM)
SM = pl.BlockSpec(memory_space=pltpu.SMEM)


def silu_of_half(h):
    return h + h * jnp.tanh(h)


def split(v):
    high = v.astype(BF16)
    return high, (v - high.astype(F32)).astype(BF16)


def segment_end(count_ref, length):
    return count_ref[lax.axis_index("grp")] * BLOCK - lax.axis_index("seq") * length


def prepare_kernel(
    width, count_ref, step_ref, sbias_ref, proj_ref, tri_ref, dt_ref, run_ref, b_ref, c_ref
):
    length, channels = step_ref.shape
    groups = length // NSTATE
    seg_end = segment_end(count_ref, length)

    @pl.when(pl.program_id(0) == 0)
    def _():
        b_rows = proj_ref[0].astype(F32)
        for t in range(length):
            b_ref[t] = jnp.broadcast_to(b_rows[:, t : t + 1], (NSTATE, LANES))
        wide = NSTATE * NSTATE
        spread = lax.broadcasted_iota(jnp.int32, (NSTATE, wide), 1) % NSTATE
        spread = (spread == lax.broadcasted_iota(jnp.int32, (NSTATE, wide), 0)).astype(BF16)
        tiled = lax.dot_general(
            proj_ref[1], spread, (((0,), (0,)), ((), ())), preferred_element_type=F32
        )
        row = lax.broadcasted_iota(jnp.int32, (length, wide), 0) % NSTATE
        col = lax.broadcasted_iota(jnp.int32, (length, wide), 1) // NSTATE
        c_ref[...] = jnp.where(row == col, tiled, 0.0).astype(BF16).reshape(groups, NSTATE, wide)

    live = lax.broadcasted_iota(jnp.int32, (length, width), 0) < seg_end
    for lane in range(0, channels, width):
        cut = pl.ds(lane, width)
        e = jnp.exp2(step_ref[:, cut].astype(F32) * LOG2E + sbias_ref[:, cut] * LOG2E)
        dt = jnp.where(e < 2e-3, e - 0.5 * e * e, jnp.log(1.0 + e))
        dt = jnp.where(live, dt, 0.0)
        dt_ref[:, :, cut] = dt.reshape(groups, NSTATE, width)
        high, low = split(dt)
        run = jnp.dot(
            tri_ref[...], jnp.concatenate([high, low], axis=0), preferred_element_type=F32
        )
        run_ref[:, :, cut] = run.reshape(groups, NSTATE, width)


def prepare(count, step, sbias, proj, pieces, width=512):
    length, channels = step.shape
    groups = length // NSTATE
    piece = channels // pieces
    tri = np.tril(np.ones((length, length), np.float32))
    tri = jnp.asarray(np.concatenate([tri, tri], axis=1), BF16)
    blocks = pl.BlockSpec((groups, NSTATE, piece), lambda j: (0, 0, j))
    whole = lambda shape: pl.BlockSpec(shape, lambda j: (0,) * len(shape))
    b_shape = (length, NSTATE, LANES)
    c_shape = (groups, NSTATE, NSTATE * NSTATE)
    return pl.pallas_call(
        functools.partial(prepare_kernel, width),
        grid=(pieces,),
        in_specs=[
            SM,
            pl.BlockSpec((length, piece), lambda j: (0, j)),
            pl.BlockSpec((1, piece), lambda j: (0, j)),
            whole(proj.shape),
            whole(tri.shape),
        ],
        out_specs=[blocks, blocks, whole(b_shape), whole(c_shape)],
        out_shape=[
            jax.ShapeDtypeStruct((groups, NSTATE, channels), F32),
            jax.ShapeDtypeStruct((groups, NSTATE, channels), F32),
            jax.ShapeDtypeStruct(b_shape, F32),
            jax.ShapeDtypeStruct(c_shape, BF16),
        ],
        compiler_params=pltpu.CompilerParams(vmem_limit_bytes=VMEM_BYTES),
        cost_estimate=pl.CostEstimate(
            flops=20 * length * channels,
            bytes_accessed=10 * length * channels,
            transcendentals=2 * length * channels,
        ),
        name="prepare",
    )(count, step, sbias, proj, tri)


def scan_kernel(
    width,
    count_ref,
    x_ref,
    halo_ref,
    dt_ref,
    run_ref,
    log_ref,
    cw_ref,
    cbias_ref,
    skip_ref,
    b_ref,
    c_ref,
    shift_ref,
    out_ref,
    msg_ref,
    drive_s,
    rate_s,
):
    length, channels = x_ref.shape
    groups = length // NSTATE
    seg_end = segment_end(count_ref, length)
    held = jnp.logical_and(seg_end >= 1, seg_end <= length).astype(F32)
    tail_at = pl.multiple_of(jnp.clip(seg_end - NSTATE, 0, length - NSTATE), NSTATE)

    for lane in range(0, channels, width):
        cut = pl.ds(lane, width)
        x = x_ref[:, cut]
        moved = jnp.dot(
            shift_ref[...],
            jnp.concatenate([x, halo_ref[:, cut]], axis=0),
            preferred_element_type=F32,
        )
        half_w = 0.5 * cw_ref[:, cut]
        half = 0.5 * cbias_ref[:, cut] + half_w[KCONV - 1 :] * x.astype(F32)
        for k in range(KCONV - 1):
            half = half + half_w[k : k + 1] * moved[k * length : (k + 1) * length]
        driven = silu_of_half(half).reshape(groups, NSTATE, width)
        drive_s[...] = dt_ref[:, :, cut] * driven
        out_ref[:, :, cut] = skip_ref[:, cut] * driven
        rate_s[...] = -LOG2E * jnp.exp(log_ref[:, cut])

        def one_group(i, state):
            rates = rate_s[...]
            mixes = []
            for tt in range(NSTATE):
                dt_now = dt_ref[i, pl.ds(tt, 1), cut]
                drive_now = drive_s[i, pl.ds(tt, 1), :]
                b_now = jnp.concatenate([b_ref[i * NSTATE + tt]] * (width // LANES), axis=1)
                state = jnp.exp2(dt_now * rates) * state + drive_now * b_now
                mixes.append(state.astype(BF16))
            out_ref[i, :, cut] += jnp.dot(
                c_ref[i], jnp.concatenate(mixes, axis=0), preferred_element_type=F32
            )
            return state

        state = lax.fori_loop(0, groups, one_group, jnp.zeros((NSTATE, width), F32))
        msg_ref[0, pl.ds(0, NSTATE), cut] = state.astype(BF16)
        s_high, s_low = split(run_ref[0, pl.ds(NSTATE - 1, 1), cut])
        tail = x_ref[pl.ds(tail_at, NSTATE), cut].astype(F32) * held
        extra = jnp.concatenate(
            [
                s_high.astype(F32),
                s_low.astype(F32),
                tail[NSTATE - (KCONV - 1) :],
                jnp.zeros((MSG - NSTATE - 2 - (KCONV - 1), width), F32),
            ],
            axis=0,
        )
        msg_ref[0, pl.ds(NSTATE, MSG - NSTATE), cut] = extra.astype(BF16)


def local_scan(count, x, halo, dt, run, log, cw, cbias, skip, b_wide, c_diag, pieces, width=512):
    length, channels = x.shape
    groups = length // NSTATE
    piece = channels // pieces
    rim = halo.shape[0]
    shift = np.zeros(((KCONV - 1) * length, length + rim), np.float32)
    for k in range(KCONV - 1):
        for t in range(length):
            source = t - (KCONV - 1) + k
            shift[k * length + t, source if source >= 0 else length + rim + source] = 1.0
    shift = jnp.asarray(shift, BF16)
    per = lambda rows: pl.BlockSpec((rows, piece), lambda j: (0, j))
    blocks = pl.BlockSpec((groups, NSTATE, piece), lambda j: (0, 0, j))
    whole = lambda a: pl.BlockSpec(a.shape, lambda j: (0,) * a.ndim)
    return pl.pallas_call(
        functools.partial(scan_kernel, width),
        grid=(pieces,),
        in_specs=[
            SM,
            per(length),
            per(rim),
            blocks,
            pl.BlockSpec((1, NSTATE, piece), lambda j: (groups - 1, 0, j)),
            per(NSTATE),
            per(KCONV),
            per(1),
            per(1),
            whole(b_wide),
            whole(c_diag),
            whole(shift),
        ],
        out_specs=[blocks, pl.BlockSpec((1, MSG, piece), lambda j: (j, 0, 0))],
        out_shape=[
            jax.ShapeDtypeStruct((groups, NSTATE, channels), F32),
            jax.ShapeDtypeStruct((pieces, MSG, piece), BF16),
        ],
        scratch_shapes=[
            pltpu.VMEM((groups, NSTATE, width), F32),
            pltpu.VMEM((NSTATE, width), F32),
        ],
        compiler_params=pltpu.CompilerParams(vmem_limit_bytes=VMEM_BYTES),
        cost_estimate=pl.CostEstimate(
            flops=8 * length * channels * NSTATE,
            bytes_accessed=12 * length * channels,
            transcendentals=length * channels * NSTATE,
        ),
        name="local_scan",
    )(count, x, halo, dt, run, log, cw, cbias, skip, b_wide, c_diag, shift)


def chain_kernel(dest_ref, got_ref, log_ref, start_ref, final_ref):
    pieces, _, piece = got_ref.shape
    own = pl.ds(pl.multiple_of(lax.axis_index("seq") * piece, piece), piece)
    rates = -LOG2E * jnp.exp(log_ref[:, own])
    state = jnp.zeros((NSTATE, piece), F32)
    tails = jnp.zeros((NSTATE, piece), F32)
    for r in range(pieces):
        start_ref[r] = state.astype(BF16)
        extra = got_ref[r, pl.ds(NSTATE, MSG - NSTATE), :].astype(F32)
        total = extra[0:1] + extra[1:2]
        state = jnp.exp2(total * rates) * state + got_ref[r, pl.ds(0, NSTATE), :].astype(F32)
        tails = tails + extra
    final_ref[...] = jnp.zeros_like(final_ref)
    dest = dest_ref[lax.axis_index("grp")]
    final_ref[dest, pl.ds(0, NSTATE), :] = state.astype(BF16)
    final_ref[dest, pl.ds(NSTATE, MSG - NSTATE), :] = tails.astype(BF16)


def chain(decode_device, got, log, groups):
    pieces, _, piece = got.shape
    return pl.pallas_call(
        chain_kernel,
        in_specs=[SM, VM(), VM()],
        out_specs=[VM(), VM()],
        out_shape=[
            jax.ShapeDtypeStruct((pieces, NSTATE, piece), BF16),
            jax.ShapeDtypeStruct((groups, MSG, piece), BF16),
        ],
        compiler_params=pltpu.CompilerParams(vmem_limit_bytes=VMEM_BYTES),
        name="chain",
    )(decode_device, got, log)


def finish_kernel(
    width, count_ref, start_ref, out_ref, run_ref, log_ref, gate_ref, c_ref, mixed_ref, rate_s, start_s
):
    length, channels = gate_ref.shape
    groups = length // NSTATE
    seg_end = segment_end(count_ref, length)
    for lane in range(0, channels, width):
        cut = pl.ds(lane, width)
        rate_s[...] = -LOG2E * jnp.exp(log_ref[:, cut])
        start_s[...] = start_ref[0, :, cut].astype(F32)

        def one_group(i, carry):
            rates, start = rate_s[...], start_s[...]
            mixes = []
            for tt in range(NSTATE):
                power = run_ref[i, pl.ds(tt, 1), cut] * rates
                mixes.append((jnp.exp2(power) * start).astype(BF16))
            carried = jnp.dot(
                c_ref[i], jnp.concatenate(mixes, axis=0), preferred_element_type=F32
            )
            rows = pl.ds(pl.multiple_of(i * NSTATE, NSTATE), NSTATE)
            gate = silu_of_half(0.5 * gate_ref[rows, cut].astype(F32))
            mixed = (out_ref[i, :, cut] + carried) * gate
            at = lax.broadcasted_iota(jnp.int32, (NSTATE, width), 0) + i * NSTATE
            mixed_ref[rows, cut] = jnp.where(at < seg_end, mixed, 0.0).astype(BF16)
            return carry

        lax.fori_loop(0, groups, one_group, 0)


def finish(count, start, out, run, log, gate, c_diag, width=512):
    length, channels = gate.shape
    groups = length // NSTATE
    pieces, _, piece = start.shape
    per = lambda rows: pl.BlockSpec((rows, piece), lambda j: (0, j))
    blocks = pl.BlockSpec((groups, NSTATE, piece), lambda j: (0, 0, j))
    return pl.pallas_call(
        functools.partial(finish_kernel, width),
        grid=(pieces,),
        in_specs=[
            SM,
            pl.BlockSpec((1, NSTATE, piece), lambda j: (j, 0, 0)),
            blocks,
            blocks,
            per(NSTATE),
            per(length),
            pl.BlockSpec(c_diag.shape, lambda j: (0, 0, 0)),
        ],
        out_specs=per(length),
        out_shape=jax.ShapeDtypeStruct((length, channels), BF16),
        scratch_shapes=[pltpu.VMEM((NSTATE, width), F32), pltpu.VMEM((NSTATE, width), F32)],
        compiler_params=pltpu.CompilerParams(vmem_limit_bytes=VMEM_BYTES),
        cost_estimate=pl.CostEstimate(
            flops=4 * length * channels * NSTATE,
            bytes_accessed=12 * length * channels,
            transcendentals=length * channels * NSTATE,
        ),
        name="finish",
    )(count, start, out, run, log, gate, c_diag)


def caches_kernel(dest_ref, got_ref, state_ref, rows_ref):
    groups = got_ref.shape[0]
    grp_pos = lax.axis_index("grp")
    state_ref[...] = jnp.zeros_like(state_ref)
    rows_ref[...] = jnp.zeros_like(rows_ref)

    def one(g, taken):
        mine = dest_ref[g] == grp_pos

        @pl.when(mine)
        def _():
            state_ref[taken] = got_ref[g, pl.ds(0, NSTATE), :].astype(F32)
            extra = got_ref[g, pl.ds(NSTATE, MSG - NSTATE), :]
            rows_ref[taken] = extra[2 : 2 + KCONV - 1]

        return taken + mine.astype(jnp.int32)

    lax.fori_loop(0, groups, one, jnp.int32(0))


def caches(decode_device, got):
    piece = got.shape[2]
    return pl.pallas_call(
        caches_kernel,
        in_specs=[SM, VM()],
        out_specs=[VM(), VM()],
        out_shape=[
            jax.ShapeDtypeStruct((MOST, NSTATE, piece), F32),
            jax.ShapeDtypeStruct((MOST, KCONV - 1, piece), BF16),
        ],
        compiler_params=pltpu.CompilerParams(vmem_limit_bytes=VMEM_BYTES),
        name="caches",
    )(decode_device, got)


def kv_kernel(here, dest_ref, count_ref, slot_ref, rows_ref, cache_ref, sems):
    groups = rows_ref.shape[0]
    grp_pos = lax.axis_index("grp")
    first = lax.axis_index("seq") * here
    cache_ref[...] = jnp.zeros_like(cache_ref)

    def each(act):
        def request(g, carry):
            @pl.when(dest_ref[g] == grp_pos)
            def _():
                def block(j, carry):
                    slot = slot_ref[g, first + j]
                    act(
                        pltpu.make_async_copy(
                            rows_ref.at[g, j], cache_ref.at[slot], sems.at[slot]
                        )
                    )
                    return carry

                lax.fori_loop(0, jnp.clip(count_ref[g] - first, 0, here), block, 0)

            return carry

        lax.fori_loop(0, groups, request, 0)

    each(lambda copy: copy.start())
    each(lambda copy: copy.wait())


def place_kv(decode_device, block_count, block_slot, rows, here, capacity):
    width = rows.shape[-1]
    return pl.pallas_call(
        functools.partial(kv_kernel, here),
        in_specs=[SM, SM, SM, pl.BlockSpec(memory_space=pl.ANY)],
        out_specs=VM(),
        out_shape=jax.ShapeDtypeStruct((capacity, BLOCK, width), BF16),
        scratch_shapes=[pltpu.SemaphoreType.DMA((capacity,))],
        compiler_params=pltpu.CompilerParams(vmem_limit_bytes=VMEM_BYTES),
        name="place_kv",
    )(decode_device, block_count, block_slot, rows)


def per_device(
    mamba_input,
    gate_input,
    step_raw,
    scan_proj,
    decay_log,
    step_bias,
    conv_weight,
    conv_bias,
    skip_gain,
    kv_rows,
    decode_device,
    block_count,
    block_slot,
):
    seg_len, channels = mamba_input.shape[1:]
    groups = lax.axis_size("grp")
    pieces = lax.axis_size("seq")
    here = seg_len // BLOCK
    x = mamba_input[0]

    kv_all = lax.all_gather(kv_rows[0].reshape(here, BLOCK, kv_rows.shape[2]), "grp")
    halo = lax.ppermute(x[seg_len - RIM :], "seq", [(s, s + 1) for s in range(pieces - 1)])
    dt, run, b_wide, c_diag = prepare(
        block_count, step_raw[0], step_bias[None], scan_proj[0], pieces
    )
    out, msg = local_scan(
        block_count,
        x,
        halo,
        dt,
        run,
        decay_log,
        conv_weight,
        conv_bias[None],
        skip_gain[None],
        b_wide,
        c_diag,
        pieces,
    )
    got = lax.all_to_all(msg, "seq", split_axis=0, concat_axis=0, tiled=True)
    starts, final = chain(decode_device, got, decay_log, groups)
    start = lax.all_to_all(starts, "seq", split_axis=0, concat_axis=0, tiled=True)
    final_got = lax.all_to_all(final, "grp", split_axis=0, concat_axis=0, tiled=True)
    block_out = finish(block_count, start, out, run, decay_log, gate_input[0], c_diag)
    ssm_cache, conv_cache = caches(decode_device, final_got)
    kv_cache = place_kv(decode_device, block_count, block_slot, kv_all, here, MOST * here)
    return block_out[None], kv_cache[None, None], ssm_cache[None], conv_cache[None]


def solution(mesh):
    return jax.shard_map(
        per_device,
        mesh=mesh,
        in_specs=(
            P("grp", "seq", None),
            P("grp", "seq", None),
            P("grp", "seq", None),
            P("grp", None, None, "seq"),
            P(),
            P(),
            P(),
            P(),
            P(),
            P("grp", "seq", None),
            P(),
            P(),
            P(),
        ),
        out_specs=(
            P("grp", "seq", None),
            P("grp", "seq", None, None, None),
            P("grp", None, None, "seq"),
            P("grp", None, None, "seq"),
        ),
        check_vma=False,
    )
```

```python
import functools

import jax
import jax.numpy as jnp
import numpy as np
from jax import lax
from jax.experimental import pallas as pl
from jax.experimental.pallas import tpu as pltpu
from jax.sharding import PartitionSpec as P

NSTATE = 16
KCONV = 4
BLOCK = 16
MOST = 3
LANES = 128
RIM = 8
LOG2E = 1.4426950408889634
MSG = 24
VMEM_BYTES = 62 * 1024 * 1024
F32 = jnp.float32
BF16 = jnp.bfloat16

VM = functools.partial(pl.BlockSpec, memory_space=pltpu.VMEM)
SM = pl.BlockSpec(memory_space=pltpu.SMEM)


def silu_of_half(h):
    return h + h * jnp.tanh(h)


def split(v):
    high = v.astype(BF16)
    return high, (v - high.astype(F32)).astype(BF16)


def segment_end(count_ref, length):
    return count_ref[lax.axis_index("grp")] * BLOCK - lax.axis_index("seq") * length


def prepare_kernel(
    width, count_ref, step_ref, sbias_ref, proj_ref, tri_ref, dt_ref, run_ref, b_ref, c_ref
):
    length, channels = step_ref.shape
    groups = length // NSTATE
    seg_end = segment_end(count_ref, length)

    @pl.when(pl.program_id(0) == 0)
    def _():
        b_rows = proj_ref[0].astype(F32)
        for t in range(length):
            b_ref[t] = jnp.broadcast_to(b_rows[:, t : t + 1], (NSTATE, LANES))
        wide = NSTATE * NSTATE
        spread = lax.broadcasted_iota(jnp.int32, (NSTATE, wide), 1) % NSTATE
        spread = (spread == lax.broadcasted_iota(jnp.int32, (NSTATE, wide), 0)).astype(BF16)
        tiled = lax.dot_general(
            proj_ref[1], spread, (((0,), (0,)), ((), ())), preferred_element_type=F32
        )
        row = lax.broadcasted_iota(jnp.int32, (length, wide), 0) % NSTATE
        col = lax.broadcasted_iota(jnp.int32, (length, wide), 1) // NSTATE
        c_ref[...] = jnp.where(row == col, tiled, 0.0).astype(BF16).reshape(groups, NSTATE, wide)

    live = lax.broadcasted_iota(jnp.int32, (length, width), 0) < seg_end
    for lane in range(0, channels, width):
        cut = pl.ds(lane, width)
        e = jnp.exp2(step_ref[:, cut].astype(F32) * LOG2E + sbias_ref[:, cut] * LOG2E)
        dt = jnp.where(e < 2e-3, e - 0.5 * e * e, jnp.log(1.0 + e))
        dt = jnp.where(live, dt, 0.0)
        dt_ref[:, :, cut] = dt.reshape(groups, NSTATE, width)
        high, low = split(dt)
        run = jnp.dot(
            tri_ref[...], jnp.concatenate([high, low], axis=0), preferred_element_type=F32
        )
        run_ref[:, :, cut] = run.reshape(groups, NSTATE, width)


def prepare(count, step, sbias, proj, pieces, width=512):
    length, channels = step.shape
    groups = length // NSTATE
    piece = channels // pieces
    tri = np.tril(np.ones((length, length), np.float32))
    tri = jnp.asarray(np.concatenate([tri, tri], axis=1), BF16)
    blocks = pl.BlockSpec((groups, NSTATE, piece), lambda j: (0, 0, j))
    whole = lambda shape: pl.BlockSpec(shape, lambda j: (0,) * len(shape))
    b_shape = (length, NSTATE, LANES)
    c_shape = (groups, NSTATE, NSTATE * NSTATE)
    return pl.pallas_call(
        functools.partial(prepare_kernel, width),
        grid=(pieces,),
        in_specs=[
            SM,
            pl.BlockSpec((length, piece), lambda j: (0, j)),
            pl.BlockSpec((1, piece), lambda j: (0, j)),
            whole(proj.shape),
            whole(tri.shape),
        ],
        out_specs=[blocks, blocks, whole(b_shape), whole(c_shape)],
        out_shape=[
            jax.ShapeDtypeStruct((groups, NSTATE, channels), F32),
            jax.ShapeDtypeStruct((groups, NSTATE, channels), F32),
            jax.ShapeDtypeStruct(b_shape, F32),
            jax.ShapeDtypeStruct(c_shape, BF16),
        ],
        compiler_params=pltpu.CompilerParams(vmem_limit_bytes=VMEM_BYTES),
        cost_estimate=pl.CostEstimate(
            flops=20 * length * channels,
            bytes_accessed=10 * length * channels,
            transcendentals=2 * length * channels,
        ),
        name="prepare",
    )(count, step, sbias, proj, tri)


def scan_kernel(
    width,
    count_ref,
    x_ref,
    halo_ref,
    dt_ref,
    run_ref,
    log_ref,
    cw_ref,
    cbias_ref,
    skip_ref,
    b_ref,
    c_ref,
    shift_ref,
    out_ref,
    msg_ref,
    drive_s,
    rate_s,
):
    length, channels = x_ref.shape
    groups = length // NSTATE
    seg_end = segment_end(count_ref, length)
    held = jnp.logical_and(seg_end >= 1, seg_end <= length).astype(F32)
    tail_at = pl.multiple_of(jnp.clip(seg_end - NSTATE, 0, length - NSTATE), NSTATE)

    for lane in range(0, channels, width):
        cut = pl.ds(lane, width)
        x = x_ref[:, cut]
        moved = jnp.dot(
            shift_ref[...],
            jnp.concatenate([x, halo_ref[:, cut]], axis=0),
            preferred_element_type=F32,
        )
        half_w = 0.5 * cw_ref[:, cut]
        half = 0.5 * cbias_ref[:, cut] + half_w[KCONV - 1 :] * x.astype(F32)
        for k in range(KCONV - 1):
            half = half + half_w[k : k + 1] * moved[k * length : (k + 1) * length]
        driven = silu_of_half(half).reshape(groups, NSTATE, width)
        drive_s[...] = dt_ref[:, :, cut] * driven
        out_ref[:, :, cut] = skip_ref[:, cut] * driven
        rate_s[...] = -LOG2E * jnp.exp(log_ref[:, cut])

        def one_group(i, state):
            rates = rate_s[...]
            mixes = []
            for tt in range(NSTATE):
                dt_now = dt_ref[i, pl.ds(tt, 1), cut]
                drive_now = drive_s[i, pl.ds(tt, 1), :]
                b_now = jnp.concatenate([b_ref[i * NSTATE + tt]] * (width // LANES), axis=1)
                state = jnp.exp2(dt_now * rates) * state + drive_now * b_now
                mixes.append(state.astype(BF16))
            out_ref[i, :, cut] += jnp.dot(
                c_ref[i], jnp.concatenate(mixes, axis=0), preferred_element_type=F32
            )
            return state

        state = lax.fori_loop(0, groups, one_group, jnp.zeros((NSTATE, width), F32), unroll=True)
        s_high, s_low = split(run_ref[0, pl.ds(NSTATE - 1, 1), cut])
        tail = x_ref[pl.ds(tail_at, NSTATE), cut].astype(F32) * held
        message = jnp.concatenate(
            [
                state,
                s_high.astype(F32),
                s_low.astype(F32),
                tail[NSTATE - (KCONV - 1) :],
                jnp.zeros((MSG - NSTATE - 2 - (KCONV - 1), width), F32),
            ],
            axis=0,
        )
        msg_ref[0, :, cut] = message.astype(BF16)


def local_scan(count, x, halo, dt, run, log, cw, cbias, skip, b_wide, c_diag, pieces, width=512):
    length, channels = x.shape
    groups = length // NSTATE
    piece = channels // pieces
    rim = halo.shape[0]
    shift = np.zeros(((KCONV - 1) * length, length + rim), np.float32)
    for k in range(KCONV - 1):
        for t in range(length):
            source = t - (KCONV - 1) + k
            shift[k * length + t, source if source >= 0 else length + rim + source] = 1.0
    shift = jnp.asarray(shift, BF16)
    per = lambda rows: pl.BlockSpec((rows, piece), lambda j: (0, j))
    blocks = pl.BlockSpec((groups, NSTATE, piece), lambda j: (0, 0, j))
    whole = lambda a: pl.BlockSpec(a.shape, lambda j: (0,) * a.ndim)
    return pl.pallas_call(
        functools.partial(scan_kernel, width),
        grid=(pieces,),
        in_specs=[
            SM,
            per(length),
            per(rim),
            blocks,
            pl.BlockSpec((1, NSTATE, piece), lambda j: (groups - 1, 0, j)),
            per(NSTATE),
            per(KCONV),
            per(1),
            per(1),
            whole(b_wide),
            whole(c_diag),
            whole(shift),
        ],
        out_specs=[blocks, pl.BlockSpec((1, MSG, piece), lambda j: (j, 0, 0))],
        out_shape=[
            jax.ShapeDtypeStruct((groups, NSTATE, channels), F32),
            jax.ShapeDtypeStruct((pieces, MSG, piece), BF16),
        ],
        scratch_shapes=[
            pltpu.VMEM((groups, NSTATE, width), F32),
            pltpu.VMEM((NSTATE, width), F32),
        ],
        compiler_params=pltpu.CompilerParams(vmem_limit_bytes=VMEM_BYTES),
        cost_estimate=pl.CostEstimate(
            flops=8 * length * channels * NSTATE,
            bytes_accessed=12 * length * channels,
            transcendentals=length * channels * NSTATE,
        ),
        name="local_scan",
    )(count, x, halo, dt, run, log, cw, cbias, skip, b_wide, c_diag, shift)


def chain_kernel(dest_ref, got_ref, log_ref, start_ref, final_ref):
    pieces, _, piece = got_ref.shape
    own = pl.ds(pl.multiple_of(lax.axis_index("seq") * piece, piece), piece)
    rates = -LOG2E * jnp.exp(log_ref[:, own])
    state = jnp.zeros((NSTATE, piece), F32)
    tails = jnp.zeros((MSG - NSTATE, piece), F32)
    for r in range(pieces):
        start_ref[r] = state.astype(BF16)
        got = got_ref[r].astype(F32)
        total = got[NSTATE : NSTATE + 1] + got[NSTATE + 1 : NSTATE + 2]
        state = jnp.exp2(total * rates) * state + got[:NSTATE]
        tails = tails + got[NSTATE:]
    final_ref[...] = jnp.zeros_like(final_ref)
    dest = dest_ref[lax.axis_index("grp")]
    final_ref[dest] = jnp.concatenate([state, tails], axis=0).astype(BF16)


def chain(decode_device, got, log, groups):
    pieces, _, piece = got.shape
    return pl.pallas_call(
        chain_kernel,
        in_specs=[SM, VM(), VM()],
        out_specs=[VM(), VM()],
        out_shape=[
            jax.ShapeDtypeStruct((pieces, NSTATE, piece), BF16),
            jax.ShapeDtypeStruct((groups, MSG, piece), BF16),
        ],
        compiler_params=pltpu.CompilerParams(vmem_limit_bytes=VMEM_BYTES),
        name="chain",
    )(decode_device, got, log)


def finish_kernel(
    width, count_ref, start_ref, out_ref, run_ref, log_ref, gate_ref, c_ref, mixed_ref, rate_s, start_s
):
    length, channels = gate_ref.shape
    groups = length // NSTATE
    seg_end = segment_end(count_ref, length)
    for lane in range(0, channels, width):
        cut = pl.ds(lane, width)
        rate_s[...] = -LOG2E * jnp.exp(log_ref[:, cut])
        start_s[...] = start_ref[0, :, cut]

        def one_group(i, carry):
            rates, start = rate_s[...], start_s[...]
            mixes = []
            for tt in range(NSTATE):
                power = (run_ref[i, pl.ds(tt, 1), cut] * rates).astype(BF16)
                mixes.append(jnp.exp2(power) * start)
            carried = jnp.dot(
                c_ref[i], jnp.concatenate(mixes, axis=0), preferred_element_type=F32
            )
            rows = pl.ds(pl.multiple_of(i * NSTATE, NSTATE), NSTATE)
            gate = silu_of_half(0.5 * gate_ref[rows, cut].astype(F32))
            mixed = (out_ref[i, :, cut] + carried) * gate
            at = lax.broadcasted_iota(jnp.int32, (NSTATE, width), 0) + i * NSTATE
            mixed_ref[rows, cut] = jnp.where(at < seg_end, mixed, 0.0).astype(BF16)
            return carry

        lax.fori_loop(0, groups, one_group, 0, unroll=True)


def finish(count, start, out, run, log, gate, c_diag, width=512):
    length, channels = gate.shape
    groups = length // NSTATE
    pieces, _, piece = start.shape
    per = lambda rows: pl.BlockSpec((rows, piece), lambda j: (0, j))
    blocks = pl.BlockSpec((groups, NSTATE, piece), lambda j: (0, 0, j))
    return pl.pallas_call(
        functools.partial(finish_kernel, width),
        grid=(pieces,),
        in_specs=[
            SM,
            pl.BlockSpec((1, NSTATE, piece), lambda j: (j, 0, 0)),
            blocks,
            blocks,
            per(NSTATE),
            per(length),
            pl.BlockSpec(c_diag.shape, lambda j: (0, 0, 0)),
        ],
        out_specs=per(length),
        out_shape=jax.ShapeDtypeStruct((length, channels), BF16),
        scratch_shapes=[pltpu.VMEM((NSTATE, width), F32), pltpu.VMEM((NSTATE, width), BF16)],
        compiler_params=pltpu.CompilerParams(vmem_limit_bytes=VMEM_BYTES),
        cost_estimate=pl.CostEstimate(
            flops=4 * length * channels * NSTATE,
            bytes_accessed=12 * length * channels,
            transcendentals=length * channels * NSTATE,
        ),
        name="finish",
    )(count, start, out, run, log, gate, c_diag)


def caches_kernel(dest_ref, got_ref, state_ref, rows_ref):
    groups = got_ref.shape[0]
    grp_pos = lax.axis_index("grp")
    state_ref[...] = jnp.zeros_like(state_ref)
    rows_ref[...] = jnp.zeros_like(rows_ref)

    def one(g, taken):
        mine = dest_ref[g] == grp_pos

        @pl.when(mine)
        def _():
            got = got_ref[g].astype(F32)
            state_ref[taken] = got[:NSTATE]
            rows_ref[taken] = got[NSTATE + 2 : NSTATE + 1 + KCONV].astype(BF16)

        return taken + mine.astype(jnp.int32)

    lax.fori_loop(0, groups, one, jnp.int32(0))


def caches(decode_device, got):
    piece = got.shape[2]
    return pl.pallas_call(
        caches_kernel,
        in_specs=[SM, VM()],
        out_specs=[VM(), VM()],
        out_shape=[
            jax.ShapeDtypeStruct((MOST, NSTATE, piece), F32),
            jax.ShapeDtypeStruct((MOST, KCONV - 1, piece), BF16),
        ],
        compiler_params=pltpu.CompilerParams(vmem_limit_bytes=VMEM_BYTES),
        name="caches",
    )(decode_device, got)


def kv_kernel(here, dest_ref, count_ref, slot_ref, rows_ref, cache_ref, sems):
    groups = rows_ref.shape[0]
    grp_pos = lax.axis_index("grp")
    first = lax.axis_index("seq") * here
    cache_ref[...] = jnp.zeros_like(cache_ref)

    def each(act):
        def request(g, carry):
            @pl.when(dest_ref[g] == grp_pos)
            def _():
                def block(j, carry):
                    slot = slot_ref[g, first + j]
                    act(
                        pltpu.make_async_copy(
                            rows_ref.at[g, j], cache_ref.at[slot], sems.at[slot]
                        )
                    )
                    return carry

                lax.fori_loop(0, jnp.clip(count_ref[g] - first, 0, here), block, 0)

            return carry

        lax.fori_loop(0, groups, request, 0)

    each(lambda copy: copy.start())
    each(lambda copy: copy.wait())


def place_kv(decode_device, block_count, block_slot, rows, here, capacity):
    width = rows.shape[-1]
    return pl.pallas_call(
        functools.partial(kv_kernel, here),
        in_specs=[SM, SM, SM, pl.BlockSpec(memory_space=pl.ANY)],
        out_specs=VM(),
        out_shape=jax.ShapeDtypeStruct((capacity, BLOCK, width), BF16),
        scratch_shapes=[pltpu.SemaphoreType.DMA((capacity,))],
        compiler_params=pltpu.CompilerParams(vmem_limit_bytes=VMEM_BYTES),
        name="place_kv",
    )(decode_device, block_count, block_slot, rows)


def per_device(
    mamba_input,
    gate_input,
    step_raw,
    scan_proj,
    decay_log,
    step_bias,
    conv_weight,
    conv_bias,
    skip_gain,
    kv_rows,
    decode_device,
    block_count,
    block_slot,
):
    seg_len, channels = mamba_input.shape[1:]
    groups = lax.axis_size("grp")
    pieces = lax.axis_size("seq")
    here = seg_len // BLOCK
    x = mamba_input[0]

    kv_all = lax.all_gather(kv_rows[0].reshape(here, BLOCK, kv_rows.shape[2]), "grp")
    halo = lax.ppermute(x[seg_len - RIM :], "seq", [(s, s + 1) for s in range(pieces - 1)])
    dt, run, b_wide, c_diag = prepare(
        block_count, step_raw[0], step_bias[None], scan_proj[0], pieces
    )
    out, msg = local_scan(
        block_count,
        x,
        halo,
        dt,
        run,
        decay_log,
        conv_weight,
        conv_bias[None],
        skip_gain[None],
        b_wide,
        c_diag,
        pieces,
    )
    got = lax.all_to_all(msg, "seq", split_axis=0, concat_axis=0, tiled=True)
    starts, final = chain(decode_device, got, decay_log, groups)
    start = lax.all_to_all(starts, "seq", split_axis=0, concat_axis=0, tiled=True)
    final_got = lax.all_to_all(final, "grp", split_axis=0, concat_axis=0, tiled=True)
    block_out = finish(block_count, start, out, run, decay_log, gate_input[0], c_diag)
    ssm_cache, conv_cache = caches(decode_device, final_got)
    kv_cache = place_kv(decode_device, block_count, block_slot, kv_all, here, MOST * here)
    return block_out[None], kv_cache[None, None], ssm_cache[None], conv_cache[None]


def solution(mesh):
    return jax.shard_map(
        per_device,
        mesh=mesh,
        in_specs=(
            P("grp", "seq", None),
            P("grp", "seq", None),
            P("grp", "seq", None),
            P("grp", None, None, "seq"),
            P(),
            P(),
            P(),
            P(),
            P(),
            P("grp", "seq", None),
            P(),
            P(),
            P(),
        ),
        out_specs=(
            P("grp", "seq", None),
            P("grp", "seq", None, None, None),
            P("grp", None, None, "seq"),
            P("grp", None, None, "seq"),
        ),
        check_vma=False,
    )
```

```python
import functools

import jax
import jax.numpy as jnp
import numpy as np
from jax import lax
from jax.experimental import pallas as pl
from jax.experimental.pallas import tpu as pltpu
from jax.sharding import PartitionSpec as P

NSTATE = 16
KCONV = 4
BLOCK = 16
MOST = 3
LANES = 128
RIM = 8
STEPS = 8
LOG2E = 1.4426950408889634
MSG = 24
VMEM_BYTES = 62 * 1024 * 1024
F32 = jnp.float32
BF16 = jnp.bfloat16

VM = functools.partial(pl.BlockSpec, memory_space=pltpu.VMEM)
SM = pl.BlockSpec(memory_space=pltpu.SMEM)


def silu_of_half(h):
    return h + h * jnp.tanh(h)


def split(v):
    high = v.astype(BF16)
    return high, (v - high.astype(F32)).astype(BF16)


def segment_end(count_ref, length):
    return count_ref[lax.axis_index("grp")] * BLOCK - lax.axis_index("seq") * length


def prepare_kernel(
    width, count_ref, step_ref, sbias_ref, proj_ref, dt_ref, b_ref, c_ref
):
    length, channels = step_ref.shape
    groups = length // NSTATE
    seg_end = segment_end(count_ref, length)

    @pl.when(pl.program_id(0) == 0)
    def _():
        b_rows = proj_ref[0].astype(F32)
        for t in range(length):
            b_ref[t] = jnp.broadcast_to(b_rows[:, t : t + 1], (NSTATE, LANES))
        wide = NSTATE * NSTATE
        spread = lax.broadcasted_iota(jnp.int32, (NSTATE, wide), 1) % NSTATE
        spread = (spread == lax.broadcasted_iota(jnp.int32, (NSTATE, wide), 0)).astype(BF16)
        tiled = lax.dot_general(
            proj_ref[1], spread, (((0,), (0,)), ((), ())), preferred_element_type=F32
        )
        row = lax.broadcasted_iota(jnp.int32, (length, wide), 0) % NSTATE
        col = lax.broadcasted_iota(jnp.int32, (length, wide), 1) // NSTATE
        c_ref[...] = jnp.where(row == col, tiled, 0.0).astype(BF16).reshape(groups, NSTATE, wide)

    live = lax.broadcasted_iota(jnp.int32, (length, width), 0) < seg_end
    for lane in range(0, channels, width):
        cut = pl.ds(lane, width)
        e = jnp.exp2(step_ref[:, cut].astype(F32) * LOG2E + sbias_ref[:, cut] * LOG2E)
        dt = jnp.where(e < 2e-3, e - 0.5 * e * e, jnp.log(1.0 + e))
        dt = jnp.where(live, dt, 0.0)
        dt_ref[:, :, cut] = dt.reshape(groups, NSTATE, width)


def prepare(count, step, sbias, proj, steps, width=512):
    length, channels = step.shape
    groups = length // NSTATE
    piece = channels // steps
    blocks = pl.BlockSpec((groups, NSTATE, piece), lambda j: (0, 0, j))
    whole = lambda shape: pl.BlockSpec(shape, lambda j: (0,) * len(shape))
    b_shape = (length, NSTATE, LANES)
    c_shape = (groups, NSTATE, NSTATE * NSTATE)
    return pl.pallas_call(
        functools.partial(prepare_kernel, width),
        grid=(steps,),
        in_specs=[
            SM,
            pl.BlockSpec((length, piece), lambda j: (0, j)),
            pl.BlockSpec((1, piece), lambda j: (0, j)),
            whole(proj.shape),
        ],
        out_specs=[blocks, whole(b_shape), whole(c_shape)],
        out_shape=[
            jax.ShapeDtypeStruct((groups, NSTATE, channels), F32),
            jax.ShapeDtypeStruct(b_shape, F32),
            jax.ShapeDtypeStruct(c_shape, BF16),
        ],
        compiler_params=pltpu.CompilerParams(vmem_limit_bytes=VMEM_BYTES),
        cost_estimate=pl.CostEstimate(
            flops=20 * length * channels,
            bytes_accessed=10 * length * channels,
            transcendentals=2 * length * channels,
        ),
        name="prepare",
    )(count, step, sbias, proj)


def scan_kernel(
    width,
    count_ref,
    x_ref,
    halo_ref,
    dt_ref,
    log_ref,
    cw_ref,
    cbias_ref,
    skip_ref,
    b_ref,
    c_ref,
    shift_ref,
    tri_ref,
    out_ref,
    run_ref,
    msg_ref,
    drive_s,
    rate_s,
):
    length, channels = x_ref.shape
    groups = length // NSTATE
    seg_end = segment_end(count_ref, length)
    held = jnp.logical_and(seg_end >= 1, seg_end <= length).astype(F32)
    tail_at = pl.multiple_of(jnp.clip(seg_end - NSTATE, 0, length - NSTATE), NSTATE)

    base = pl.program_id(0) * channels
    piece = msg_ref.shape[2]

    def tile(l, carry):
        cut = pl.ds(pl.multiple_of(l * width, width), width)
        at = pl.ds(pl.multiple_of(base + l * width, width), width)
        x = x_ref[:, cut]
        moved = jnp.dot(
            shift_ref[...],
            jnp.concatenate([x, halo_ref[:, at]], axis=0),
            preferred_element_type=F32,
        )
        half_w = 0.5 * cw_ref[:, at]
        half = 0.5 * cbias_ref[:, at] + half_w[KCONV - 1 :] * x.astype(F32)
        for k in range(KCONV - 1):
            half = half + half_w[k : k + 1] * moved[k * length : (k + 1) * length]
        driven = silu_of_half(half).reshape(groups, NSTATE, width)
        dt = dt_ref[:, :, cut]
        drive_s[...] = dt * driven
        high, low = split(dt.reshape(length, width))
        run = jnp.dot(
            tri_ref[...], jnp.concatenate([high, low], axis=0), preferred_element_type=F32
        )
        run_ref[:, :, cut] = run.reshape(groups, NSTATE, width)
        out_ref[:, :, cut] = skip_ref[:, at] * driven
        rate_s[...] = -LOG2E * jnp.exp(log_ref[:, at])

        def one_group(i, state):
            rates = rate_s[...]
            mixes = []
            for tt in range(NSTATE):
                dt_now = dt_ref[i, pl.ds(tt, 1), cut]
                drive_now = drive_s[i, pl.ds(tt, 1), :]
                b_now = jnp.concatenate([b_ref[i * NSTATE + tt]] * (width // LANES), axis=1)
                state = jnp.exp2(dt_now * rates) * state + drive_now * b_now
                mixes.append(state.astype(BF16))
            out_ref[i, :, cut] += jnp.dot(
                c_ref[i], jnp.concatenate(mixes, axis=0), preferred_element_type=F32
            )
            return state

        state = lax.fori_loop(0, groups, one_group, jnp.zeros((NSTATE, width), F32), unroll=True)
        s_high, s_low = split(run[length - 1 :])
        tail = x_ref[pl.ds(tail_at, NSTATE), cut].astype(F32) * held
        message = jnp.concatenate(
            [
                state,
                s_high.astype(F32),
                s_low.astype(F32),
                tail[NSTATE - (KCONV - 1) :],
                jnp.zeros((MSG - NSTATE - 2 - (KCONV - 1), width), F32),
            ],
            axis=0,
        )
        inside = pl.ds(pl.multiple_of((l * width) % piece, width), width)
        msg_ref[(l * width) // piece, :, inside] = message.astype(BF16)
        return carry

    lax.fori_loop(0, channels // width, tile, 0)


def local_scan(
    count, x, halo, dt, log, cw, cbias, skip, b_wide, c_diag, pieces, steps, width=512
):
    length, channels = x.shape
    groups = length // NSTATE
    piece = channels // pieces
    block = channels // steps
    rim = halo.shape[0]
    shift = np.zeros(((KCONV - 1) * length, length + rim), np.float32)
    for k in range(KCONV - 1):
        for t in range(length):
            source = t - (KCONV - 1) + k
            shift[k * length + t, source if source >= 0 else length + rim + source] = 1.0
    shift = jnp.asarray(shift, BF16)
    tri = np.tril(np.ones((length, length), np.float32))
    tri = jnp.asarray(np.concatenate([tri, tri], axis=1), BF16)
    per = lambda rows: pl.BlockSpec((rows, block), lambda j: (0, j))
    blocks = pl.BlockSpec((groups, NSTATE, block), lambda j: (0, 0, j))
    whole = lambda a: pl.BlockSpec(a.shape, lambda j: (0,) * a.ndim)
    return pl.pallas_call(
        functools.partial(scan_kernel, width),
        grid=(steps,),
        in_specs=[
            SM,
            per(length),
            whole(halo),
            blocks,
            whole(log),
            whole(cw),
            whole(cbias),
            whole(skip),
            whole(b_wide),
            whole(c_diag),
            whole(shift),
            whole(tri),
        ],
        out_specs=[blocks, blocks, pl.BlockSpec((block // piece, MSG, piece), lambda j: (j, 0, 0))],
        out_shape=[
            jax.ShapeDtypeStruct((groups, NSTATE, channels), F32),
            jax.ShapeDtypeStruct((groups, NSTATE, channels), F32),
            jax.ShapeDtypeStruct((pieces, MSG, piece), BF16),
        ],
        scratch_shapes=[
            pltpu.VMEM((groups, NSTATE, width), F32),
            pltpu.VMEM((NSTATE, width), F32),
        ],
        compiler_params=pltpu.CompilerParams(vmem_limit_bytes=VMEM_BYTES),
        cost_estimate=pl.CostEstimate(
            flops=8 * length * channels * NSTATE,
            bytes_accessed=12 * length * channels,
            transcendentals=length * channels * NSTATE,
        ),
        name="local_scan",
    )(count, x, halo, dt, log, cw, cbias, skip, b_wide, c_diag, shift, tri)


def chain_kernel(dest_ref, got_ref, log_ref, start_ref, final_ref, log_s, sem):
    pieces, _, piece = got_ref.shape
    own = pl.ds(pl.multiple_of(lax.axis_index("seq") * piece, piece), piece)
    copy = pltpu.make_async_copy(log_ref.at[:, own], log_s, sem)
    copy.start()
    copy.wait()
    rates = -LOG2E * jnp.exp(log_s[...])
    state = jnp.zeros((NSTATE, piece), F32)
    tails = jnp.zeros((MSG - NSTATE, piece), F32)
    for r in range(pieces):
        start_ref[r] = state.astype(BF16)
        got = got_ref[r].astype(F32)
        total = got[NSTATE : NSTATE + 1] + got[NSTATE + 1 : NSTATE + 2]
        state = jnp.exp2(total * rates) * state + got[:NSTATE]
        tails = tails + got[NSTATE:]
    final_ref[...] = jnp.zeros_like(final_ref)
    dest = dest_ref[lax.axis_index("grp")]
    final_ref[dest] = jnp.concatenate([state, tails], axis=0).astype(BF16)


def chain(decode_device, got, log, groups):
    pieces, _, piece = got.shape
    return pl.pallas_call(
        chain_kernel,
        in_specs=[SM, VM(), pl.BlockSpec(memory_space=pl.ANY)],
        out_specs=[VM(), VM()],
        out_shape=[
            jax.ShapeDtypeStruct((pieces, NSTATE, piece), BF16),
            jax.ShapeDtypeStruct((groups, MSG, piece), BF16),
        ],
        scratch_shapes=[pltpu.VMEM((NSTATE, piece), F32), pltpu.SemaphoreType.DMA],
        compiler_params=pltpu.CompilerParams(vmem_limit_bytes=VMEM_BYTES),
        name="chain",
    )(decode_device, got, log)


def finish_kernel(
    width, count_ref, start_ref, out_ref, run_ref, log_ref, gate_ref, c_ref, mixed_ref, rate_s, start_s
):
    length, channels = gate_ref.shape
    groups = length // NSTATE
    seg_end = segment_end(count_ref, length)
    base = pl.program_id(0) * channels
    piece = start_ref.shape[2]

    def tile(l, carry):
        cut = pl.ds(pl.multiple_of(l * width, width), width)
        at = pl.ds(pl.multiple_of(base + l * width, width), width)
        inside = pl.ds(pl.multiple_of((l * width) % piece, width), width)
        rate_s[...] = (-LOG2E * jnp.exp(log_ref[:, at])).astype(BF16)
        start_s[...] = start_ref[(l * width) // piece, :, inside]

        def one_group(i, carry):
            rates, start = rate_s[...], start_s[...]
            mixes = []
            for tt in range(NSTATE):
                run_now = jnp.broadcast_to(run_ref[i, pl.ds(tt, 1), cut], (NSTATE, width))
                mixes.append(jnp.exp2(run_now.astype(BF16) * rates) * start)
            carried = jnp.dot(
                c_ref[i], jnp.concatenate(mixes, axis=0), preferred_element_type=F32
            )
            rows = pl.ds(pl.multiple_of(i * NSTATE, NSTATE), NSTATE)
            gate = silu_of_half(0.5 * gate_ref[rows, cut].astype(F32))
            mixed = (out_ref[i, :, cut] + carried) * gate
            row = lax.broadcasted_iota(jnp.int32, (NSTATE, width), 0) + i * NSTATE
            mixed_ref[rows, cut] = jnp.where(row < seg_end, mixed, 0.0).astype(BF16)
            return carry

        lax.fori_loop(0, groups, one_group, 0, unroll=True)
        return carry

    lax.fori_loop(0, channels // width, tile, 0)


def finish(count, start, out, run, log, gate, c_diag, steps, width=1024):
    length, channels = gate.shape
    groups = length // NSTATE
    pieces, _, piece = start.shape
    block = channels // steps
    per = lambda rows: pl.BlockSpec((rows, block), lambda j: (0, j))
    blocks = pl.BlockSpec((groups, NSTATE, block), lambda j: (0, 0, j))
    return pl.pallas_call(
        functools.partial(finish_kernel, width),
        grid=(steps,),
        in_specs=[
            SM,
            pl.BlockSpec((block // piece, NSTATE, piece), lambda j: (j, 0, 0)),
            blocks,
            blocks,
            pl.BlockSpec(log.shape, lambda j: (0, 0)),
            per(length),
            pl.BlockSpec(c_diag.shape, lambda j: (0, 0, 0)),
        ],
        out_specs=per(length),
        out_shape=jax.ShapeDtypeStruct((length, channels), BF16),
        scratch_shapes=[pltpu.VMEM((NSTATE, width), BF16), pltpu.VMEM((NSTATE, width), BF16)],
        compiler_params=pltpu.CompilerParams(vmem_limit_bytes=VMEM_BYTES),
        cost_estimate=pl.CostEstimate(
            flops=4 * length * channels * NSTATE,
            bytes_accessed=12 * length * channels,
            transcendentals=length * channels * NSTATE,
        ),
        name="finish",
    )(count, start, out, run, log, gate, c_diag)


def caches_kernel(
    here,
    dest_ref,
    count_ref,
    slot_ref,
    kv_ref,
    got_ref,
    cache_ref,
    state_ref,
    rows_ref,
    got_s,
    got_sem,
    kv_sems,
):
    groups = got_ref.shape[0]
    grp_pos = lax.axis_index("grp")
    first = lax.axis_index("seq") * here
    got_copy = pltpu.make_async_copy(got_ref, got_s, got_sem)
    got_copy.start()
    cache_ref[...] = jnp.zeros_like(cache_ref)

    def each_block(act):
        def request(g, carry):
            @pl.when(dest_ref[g] == grp_pos)
            def _():
                def block(j, carry):
                    slot = slot_ref[g, first + j]
                    act(
                        pltpu.make_async_copy(
                            kv_ref.at[g, j], cache_ref.at[slot], kv_sems.at[slot]
                        )
                    )
                    return carry

                lax.fori_loop(0, jnp.clip(count_ref[g] - first, 0, here), block, 0)

            return carry

        lax.fori_loop(0, groups, request, 0)

    each_block(lambda copy: copy.start())
    state_ref[...] = jnp.zeros_like(state_ref)
    rows_ref[...] = jnp.zeros_like(rows_ref)
    got_copy.wait()

    def one(g, taken):
        mine = dest_ref[g] == grp_pos

        @pl.when(mine)
        def _():
            got = got_s[g].astype(F32)
            state_ref[taken] = got[:NSTATE]
            rows_ref[taken] = got[NSTATE + 2 : NSTATE + 1 + KCONV].astype(BF16)

        return taken + mine.astype(jnp.int32)

    lax.fori_loop(0, groups, one, jnp.int32(0))
    each_block(lambda copy: copy.wait())


def caches(decode_device, block_count, block_slot, kv, got, here, capacity):
    piece = got.shape[2]
    width = kv.shape[-1]
    return pl.pallas_call(
        functools.partial(caches_kernel, here),
        in_specs=[
            SM,
            SM,
            SM,
            pl.BlockSpec(memory_space=pl.ANY),
            pl.BlockSpec(memory_space=pl.ANY),
        ],
        out_specs=[VM(), VM(), VM()],
        out_shape=[
            jax.ShapeDtypeStruct((capacity, BLOCK, width), BF16),
            jax.ShapeDtypeStruct((MOST, NSTATE, piece), F32),
            jax.ShapeDtypeStruct((MOST, KCONV - 1, piece), BF16),
        ],
        scratch_shapes=[
            pltpu.VMEM(got.shape, BF16),
            pltpu.SemaphoreType.DMA,
            pltpu.SemaphoreType.DMA((capacity,)),
        ],
        compiler_params=pltpu.CompilerParams(vmem_limit_bytes=VMEM_BYTES),
        name="caches",
    )(decode_device, block_count, block_slot, kv, got)


def per_device(
    mamba_input,
    gate_input,
    step_raw,
    scan_proj,
    decay_log,
    step_bias,
    conv_weight,
    conv_bias,
    skip_gain,
    kv_rows,
    decode_device,
    block_count,
    block_slot,
):
    seg_len, channels = mamba_input.shape[1:]
    groups = lax.axis_size("grp")
    pieces = lax.axis_size("seq")
    here = seg_len // BLOCK
    x = mamba_input[0]

    kv_all = lax.all_gather(kv_rows[0].reshape(here, BLOCK, kv_rows.shape[2]), "grp")
    halo = lax.ppermute(x[seg_len - RIM :], "seq", [(s, s + 1) for s in range(pieces - 1)])
    dt, b_wide, c_diag = prepare(block_count, step_raw[0], step_bias[None], scan_proj[0], 2)
    out, run, msg = local_scan(
        block_count,
        x,
        halo,
        dt,
        decay_log,
        conv_weight,
        conv_bias[None],
        skip_gain[None],
        b_wide,
        c_diag,
        pieces,
        STEPS,
    )
    got = lax.all_to_all(msg, "seq", split_axis=0, concat_axis=0, tiled=True)
    starts, final = chain(decode_device, got, decay_log, groups)
    start = lax.all_to_all(starts, "seq", split_axis=0, concat_axis=0, tiled=True)
    final_got = lax.all_to_all(final, "grp", split_axis=0, concat_axis=0, tiled=True)
    block_out = finish(block_count, start, out, run, decay_log, gate_input[0], c_diag, STEPS)
    kv_cache, ssm_cache, conv_cache = caches(
        decode_device, block_count, block_slot, kv_all, final_got, here, MOST * here
    )
    return block_out[None], kv_cache[None, None], ssm_cache[None], conv_cache[None]


def solution(mesh):
    return jax.shard_map(
        per_device,
        mesh=mesh,
        in_specs=(
            P("grp", "seq", None),
            P("grp", "seq", None),
            P("grp", "seq", None),
            P("grp", None, None, "seq"),
            P(),
            P(),
            P(),
            P(),
            P(),
            P("grp", "seq", None),
            P(),
            P(),
            P(),
        ),
        out_specs=(
            P("grp", "seq", None),
            P("grp", "seq", None, None, None),
            P("grp", None, None, "seq"),
            P("grp", None, None, "seq"),
        ),
        check_vma=False,
    )
```

```python
import functools

import jax
import jax.numpy as jnp
import numpy as np
from jax import lax
from jax.experimental import pallas as pl
from jax.experimental.pallas import tpu as pltpu
from jax.sharding import PartitionSpec as P

NSTATE = 16
KCONV = 4
BLOCK = 16
MOST = 3
LANES = 128
RIM = 8
STEPS = 8
LOG2E = 1.4426950408889634
LOG2LOG2E = 0.5287663729448977
MSG = 24
VMEM_BYTES = 62 * 1024 * 1024
WIDE_BYTES = 48 * 1024 * 1024
SMALL_BYTES = 16 * 1024 * 1024
F32 = jnp.float32
BF16 = jnp.bfloat16

VM = functools.partial(pl.BlockSpec, memory_space=pltpu.VMEM)
SM = pl.BlockSpec(memory_space=pltpu.SMEM)


def silu_of_half(h):
    return h + h * jnp.tanh(h)


def rate_of(log):
    return jnp.exp2(log * LOG2E + LOG2LOG2E)


def split(v):
    high = v.astype(BF16)
    return high, (v - high.astype(F32)).astype(BF16)


def segment_end(count_ref, length):
    return count_ref[lax.axis_index("grp")] * BLOCK - lax.axis_index("seq") * length


def prepare_kernel(
    width, count_ref, step_ref, sbias_ref, proj_ref, dt_ref, b_ref, c_ref
):
    length, channels = step_ref.shape
    groups = length // NSTATE
    seg_end = segment_end(count_ref, length)

    @pl.when(pl.program_id(0) == 0)
    def _():
        b_rows = proj_ref[0].astype(F32)
        for t in range(length):
            b_ref[t] = jnp.broadcast_to(-b_rows[:, t : t + 1], (NSTATE, LANES))
        wide = NSTATE * NSTATE
        spread = lax.broadcasted_iota(jnp.int32, (NSTATE, wide), 1) % NSTATE
        spread = (spread == lax.broadcasted_iota(jnp.int32, (NSTATE, wide), 0)).astype(BF16)
        tiled = lax.dot_general(
            proj_ref[1], spread, (((0,), (0,)), ((), ())), preferred_element_type=F32
        )
        row = lax.broadcasted_iota(jnp.int32, (length, wide), 0) % NSTATE
        col = lax.broadcasted_iota(jnp.int32, (length, wide), 1) // NSTATE
        c_ref[...] = jnp.where(row == col, tiled, 0.0).astype(BF16).reshape(groups, NSTATE, wide)

    live = lax.broadcasted_iota(jnp.int32, (length, width), 0) < seg_end
    for lane in range(0, channels, width):
        cut = pl.ds(lane, width)
        e = jnp.exp2(step_ref[:, cut].astype(F32) * LOG2E + sbias_ref[:, cut] * LOG2E)
        minus_dt = jnp.where(e < 2e-3, e * (0.5 * e - 1.0), -jnp.log(1.0 + e))
        minus_dt = jnp.where(live, minus_dt, 0.0)
        dt_ref[:, :, cut] = minus_dt.reshape(groups, NSTATE, width)


def prepare(count, step, sbias, proj, steps, width=512):
    length, channels = step.shape
    groups = length // NSTATE
    piece = channels // steps
    blocks = pl.BlockSpec((groups, NSTATE, piece), lambda j: (0, 0, j))
    whole = lambda shape: pl.BlockSpec(shape, lambda j: (0,) * len(shape))
    b_shape = (length, NSTATE, LANES)
    c_shape = (groups, NSTATE, NSTATE * NSTATE)
    return pl.pallas_call(
        functools.partial(prepare_kernel, width),
        grid=(steps,),
        in_specs=[
            SM,
            pl.BlockSpec((length, piece), lambda j: (0, j)),
            pl.BlockSpec((1, piece), lambda j: (0, j)),
            whole(proj.shape),
        ],
        out_specs=[blocks, whole(b_shape), whole(c_shape)],
        out_shape=[
            jax.ShapeDtypeStruct((groups, NSTATE, channels), F32),
            jax.ShapeDtypeStruct(b_shape, F32),
            jax.ShapeDtypeStruct(c_shape, BF16),
        ],
        compiler_params=pltpu.CompilerParams(vmem_limit_bytes=VMEM_BYTES),
        cost_estimate=pl.CostEstimate(
            flops=20 * length * channels,
            bytes_accessed=10 * length * channels,
            transcendentals=2 * length * channels,
        ),
        name="prepare",
    )(count, step, sbias, proj)


def scan_kernel(
    width,
    count_ref,
    x_ref,
    halo_ref,
    dt_ref,
    log_ref,
    cw_ref,
    cbias_ref,
    skip_ref,
    b_ref,
    c_ref,
    shift_ref,
    tri_ref,
    out_ref,
    run_ref,
    msg_ref,
    drive_s,
    rate_s,
):
    length, channels = x_ref.shape
    groups = length // NSTATE
    seg_end = segment_end(count_ref, length)
    held = jnp.logical_and(seg_end >= 1, seg_end <= length).astype(F32)
    tail_at = pl.multiple_of(jnp.clip(seg_end - NSTATE, 0, length - NSTATE), NSTATE)

    base = pl.program_id(0) * channels
    piece = msg_ref.shape[2]

    def tile(l, carry):
        cut = pl.ds(pl.multiple_of(l * width, width), width)
        at = pl.ds(pl.multiple_of(base + l * width, width), width)
        x = x_ref[:, cut]
        moved = jnp.dot(
            shift_ref[...],
            jnp.concatenate([x, halo_ref[:, at]], axis=0),
            preferred_element_type=F32,
        )
        half_w = 0.5 * cw_ref[:, at]
        half = 0.5 * cbias_ref[:, at] + half_w[KCONV - 1 :] * x.astype(F32)
        for k in range(KCONV - 1):
            half = half + half_w[k : k + 1] * moved[k * length : (k + 1) * length]
        driven = silu_of_half(half).reshape(groups, NSTATE, width)
        dt = dt_ref[:, :, cut]
        drive_s[...] = dt * driven
        high, low = split(dt.reshape(length, width))
        run = jnp.dot(
            tri_ref[...], jnp.concatenate([high, low], axis=0), preferred_element_type=F32
        )
        run_ref[:, :, cut] = run.reshape(groups, NSTATE, width)
        out_ref[:, :, cut] = skip_ref[:, at] * driven
        rate_s[...] = rate_of(log_ref[:, at])

        def one_group(i, state):
            rates = rate_s[...]
            mixes = []
            for tt in range(NSTATE):
                dt_now = dt_ref[i, pl.ds(tt, 1), cut]
                drive_now = drive_s[i, pl.ds(tt, 1), :]
                b_now = jnp.concatenate([b_ref[i * NSTATE + tt]] * (width // LANES), axis=1)
                state = jnp.exp2(dt_now * rates) * state + drive_now * b_now
                mixes.append(state.astype(BF16))
            out_ref[i, :, cut] += jnp.dot(
                c_ref[i], jnp.concatenate(mixes, axis=0), preferred_element_type=F32
            )
            return state

        state = lax.fori_loop(0, groups, one_group, jnp.zeros((NSTATE, width), F32), unroll=True)
        s_high, s_low = split(run[length - 1 :])
        tail = x_ref[pl.ds(tail_at, NSTATE), cut].astype(F32) * held
        message = jnp.concatenate(
            [
                state,
                s_high.astype(F32),
                s_low.astype(F32),
                tail[NSTATE - (KCONV - 1) :],
                jnp.zeros((MSG - NSTATE - 2 - (KCONV - 1), width), F32),
            ],
            axis=0,
        )
        inside = pl.ds(pl.multiple_of((l * width) % piece, width), width)
        msg_ref[(l * width) // piece, :, inside] = message.astype(BF16)
        return carry

    lax.fori_loop(0, channels // width, tile, 0)


def local_scan(
    count, x, halo, dt, log, cw, cbias, skip, b_wide, c_diag, pieces, steps, width=512
):
    length, channels = x.shape
    groups = length // NSTATE
    piece = channels // pieces
    block = channels // steps
    rim = halo.shape[0]
    shift = np.zeros(((KCONV - 1) * length, length + rim), np.float32)
    for k in range(KCONV - 1):
        for t in range(length):
            source = t - (KCONV - 1) + k
            shift[k * length + t, source if source >= 0 else length + rim + source] = 1.0
    shift = jnp.asarray(shift, BF16)
    tri = np.tril(np.ones((length, length), np.float32))
    tri = jnp.asarray(np.concatenate([tri, tri], axis=1), BF16)
    per = lambda rows: pl.BlockSpec((rows, block), lambda j: (0, j))
    blocks = pl.BlockSpec((groups, NSTATE, block), lambda j: (0, 0, j))
    whole = lambda a: pl.BlockSpec(a.shape, lambda j: (0,) * a.ndim)
    return pl.pallas_call(
        functools.partial(scan_kernel, width),
        grid=(steps,),
        in_specs=[
            SM,
            per(length),
            whole(halo),
            blocks,
            whole(log),
            whole(cw),
            whole(cbias),
            whole(skip),
            whole(b_wide),
            whole(c_diag),
            whole(shift),
            whole(tri),
        ],
        out_specs=[blocks, blocks, pl.BlockSpec((block // piece, MSG, piece), lambda j: (j, 0, 0))],
        out_shape=[
            jax.ShapeDtypeStruct((groups, NSTATE, channels), F32),
            jax.ShapeDtypeStruct((groups, NSTATE, channels), F32),
            jax.ShapeDtypeStruct((pieces, MSG, piece), BF16),
        ],
        scratch_shapes=[
            pltpu.VMEM((groups, NSTATE, width), F32),
            pltpu.VMEM((NSTATE, width), F32),
        ],
        compiler_params=pltpu.CompilerParams(vmem_limit_bytes=VMEM_BYTES),
        cost_estimate=pl.CostEstimate(
            flops=8 * length * channels * NSTATE,
            bytes_accessed=12 * length * channels,
            transcendentals=length * channels * NSTATE,
        ),
        name="local_scan",
    )(count, x, halo, dt, log, cw, cbias, skip, b_wide, c_diag, shift, tri)


def chain_kernel(dest_ref, got_ref, log_ref, start_ref, final_ref):
    pieces, _, piece = got_ref.shape
    own = pl.ds(pl.multiple_of(lax.axis_index("seq") * piece, piece), piece)
    rates = rate_of(log_ref[:, own])
    state = jnp.zeros((NSTATE, piece), F32)
    tails = jnp.zeros((MSG - NSTATE, piece), F32)
    for r in range(pieces):
        start_ref[r] = state.astype(BF16)
        got = got_ref[r].astype(F32)
        total = got[NSTATE : NSTATE + 1] + got[NSTATE + 1 : NSTATE + 2]
        state = jnp.exp2(total * rates) * state + got[:NSTATE]
        tails = tails + got[NSTATE:]
    final_ref[...] = jnp.zeros_like(final_ref)
    dest = dest_ref[lax.axis_index("grp")]
    final_ref[dest] = jnp.concatenate([state, tails], axis=0).astype(BF16)


def chain(decode_device, got, log, groups):
    pieces, _, piece = got.shape
    return pl.pallas_call(
        chain_kernel,
        in_specs=[SM, VM(), VM()],
        out_specs=[VM(), VM()],
        out_shape=[
            jax.ShapeDtypeStruct((pieces, NSTATE, piece), BF16),
            jax.ShapeDtypeStruct((groups, MSG, piece), BF16),
        ],
        compiler_params=pltpu.CompilerParams(vmem_limit_bytes=SMALL_BYTES),
        name="chain",
    )(decode_device, got, log)


def finish_kernel(
    width, count_ref, start_ref, out_ref, run_ref, log_ref, gate_ref, c_ref, mixed_ref, rate_s, start_s
):
    length, channels = gate_ref.shape
    groups = length // NSTATE
    seg_end = segment_end(count_ref, length)
    base = pl.program_id(0) * channels
    piece = start_ref.shape[2]

    def tile(l, carry):
        cut = pl.ds(pl.multiple_of(l * width, width), width)
        at = pl.ds(pl.multiple_of(base + l * width, width), width)
        inside = pl.ds(pl.multiple_of((l * width) % piece, width), width)
        rate_s[...] = rate_of(log_ref[:, at]).astype(BF16)
        start_s[...] = start_ref[(l * width) // piece, :, inside]

        def one_group(i, carry):
            rates, start = rate_s[...], start_s[...]
            mixes = []
            for tt in range(NSTATE):
                run_now = jnp.broadcast_to(run_ref[i, pl.ds(tt, 1), cut], (NSTATE, width))
                mixes.append(jnp.exp2(run_now.astype(BF16) * rates) * start)
            carried = jnp.dot(
                c_ref[i], jnp.concatenate(mixes, axis=0), preferred_element_type=F32
            )
            rows = pl.ds(pl.multiple_of(i * NSTATE, NSTATE), NSTATE)
            gate = silu_of_half(0.5 * gate_ref[rows, cut].astype(F32))
            mixed = (out_ref[i, :, cut] + carried) * gate
            row = lax.broadcasted_iota(jnp.int32, (NSTATE, width), 0) + i * NSTATE
            mixed_ref[rows, cut] = jnp.where(row < seg_end, mixed, 0.0).astype(BF16)
            return carry

        lax.fori_loop(0, groups, one_group, 0, unroll=True)
        return carry

    lax.fori_loop(0, channels // width, tile, 0)


def finish(count, start, out, run, log, gate, c_diag, steps, width=1024):
    length, channels = gate.shape
    groups = length // NSTATE
    pieces, _, piece = start.shape
    block = channels // steps
    per = lambda rows: pl.BlockSpec((rows, block), lambda j: (0, j))
    blocks = pl.BlockSpec((groups, NSTATE, block), lambda j: (0, 0, j))
    return pl.pallas_call(
        functools.partial(finish_kernel, width),
        grid=(steps,),
        in_specs=[
            SM,
            pl.BlockSpec((block // piece, NSTATE, piece), lambda j: (j, 0, 0)),
            blocks,
            blocks,
            pl.BlockSpec(log.shape, lambda j: (0, 0)),
            per(length),
            pl.BlockSpec(c_diag.shape, lambda j: (0, 0, 0)),
        ],
        out_specs=per(length),
        out_shape=jax.ShapeDtypeStruct((length, channels), BF16),
        scratch_shapes=[pltpu.VMEM((NSTATE, width), BF16), pltpu.VMEM((NSTATE, width), BF16)],
        compiler_params=pltpu.CompilerParams(vmem_limit_bytes=VMEM_BYTES),
        cost_estimate=pl.CostEstimate(
            flops=4 * length * channels * NSTATE,
            bytes_accessed=12 * length * channels,
            transcendentals=length * channels * NSTATE,
        ),
        name="finish",
    )(count, start, out, run, log, gate, c_diag)


def caches_kernel(
    here,
    dest_ref,
    count_ref,
    slot_ref,
    kv_ref,
    got_ref,
    cache_ref,
    state_ref,
    rows_ref,
    kv_sems,
):
    groups = got_ref.shape[0]
    grp_pos = lax.axis_index("grp")
    first = lax.axis_index("seq") * here
    cache_ref[...] = jnp.zeros_like(cache_ref)

    def each_block(act):
        def request(g, carry):
            @pl.when(dest_ref[g] == grp_pos)
            def _():
                def block(j, carry):
                    slot = slot_ref[g, first + j]
                    act(
                        pltpu.make_async_copy(
                            kv_ref.at[g, j], cache_ref.at[slot], kv_sems.at[slot]
                        )
                    )
                    return carry

                lax.fori_loop(0, jnp.clip(count_ref[g] - first, 0, here), block, 0)

            return carry

        lax.fori_loop(0, groups, request, 0)

    each_block(lambda copy: copy.start())
    state_ref[...] = jnp.zeros_like(state_ref)
    rows_ref[...] = jnp.zeros_like(rows_ref)

    def one(g, taken):
        mine = dest_ref[g] == grp_pos

        @pl.when(mine)
        def _():
            got = got_ref[g].astype(F32)
            state_ref[taken] = got[:NSTATE]
            rows_ref[taken] = got[NSTATE + 2 : NSTATE + 1 + KCONV].astype(BF16)

        return taken + mine.astype(jnp.int32)

    lax.fori_loop(0, groups, one, jnp.int32(0))
    each_block(lambda copy: copy.wait())


def caches(decode_device, block_count, block_slot, kv, got, here, capacity):
    piece = got.shape[2]
    width = kv.shape[-1]
    return pl.pallas_call(
        functools.partial(caches_kernel, here),
        in_specs=[
            SM,
            SM,
            SM,
            pl.BlockSpec(memory_space=pl.ANY),
            VM(),
        ],
        out_specs=[VM(), VM(), VM()],
        out_shape=[
            jax.ShapeDtypeStruct((capacity, BLOCK, width), BF16),
            jax.ShapeDtypeStruct((MOST, NSTATE, piece), F32),
            jax.ShapeDtypeStruct((MOST, KCONV - 1, piece), BF16),
        ],
        scratch_shapes=[
            pltpu.SemaphoreType.DMA((capacity,)),
        ],
        compiler_params=pltpu.CompilerParams(vmem_limit_bytes=WIDE_BYTES),
        name="caches",
    )(decode_device, block_count, block_slot, kv, got)


def per_device(
    mamba_input,
    gate_input,
    step_raw,
    scan_proj,
    decay_log,
    step_bias,
    conv_weight,
    conv_bias,
    skip_gain,
    kv_rows,
    decode_device,
    block_count,
    block_slot,
):
    seg_len, channels = mamba_input.shape[1:]
    groups = lax.axis_size("grp")
    pieces = lax.axis_size("seq")
    here = seg_len // BLOCK
    x = mamba_input[0]

    kv_all = lax.all_gather(kv_rows[0].reshape(here, BLOCK, kv_rows.shape[2]), "grp")
    halo = lax.ppermute(x[seg_len - RIM :], "seq", [(s, s + 1) for s in range(pieces - 1)])
    dt, b_wide, c_diag = prepare(block_count, step_raw[0], step_bias[None], scan_proj[0], 2)
    out, run, msg = local_scan(
        block_count,
        x,
        halo,
        dt,
        decay_log,
        conv_weight,
        conv_bias[None],
        skip_gain[None],
        b_wide,
        c_diag,
        pieces,
        STEPS,
    )
    got = lax.all_to_all(msg, "seq", split_axis=0, concat_axis=0, tiled=True)
    starts, final = chain(decode_device, got, decay_log, groups)
    start = lax.all_to_all(starts, "seq", split_axis=0, concat_axis=0, tiled=True)
    final_got = lax.all_to_all(final, "grp", split_axis=0, concat_axis=0, tiled=True)
    block_out = finish(block_count, start, out, run, decay_log, gate_input[0], c_diag, STEPS)
    kv_cache, ssm_cache, conv_cache = caches(
        decode_device, block_count, block_slot, kv_all, final_got, here, MOST * here
    )
    return block_out[None], kv_cache[None, None], ssm_cache[None], conv_cache[None]


def solution(mesh):
    return jax.shard_map(
        per_device,
        mesh=mesh,
        in_specs=(
            P("grp", "seq", None),
            P("grp", "seq", None),
            P("grp", "seq", None),
            P("grp", None, None, "seq"),
            P(),
            P(),
            P(),
            P(),
            P(),
            P("grp", "seq", None),
            P(),
            P(),
            P(),
        ),
        out_specs=(
            P("grp", "seq", None),
            P("grp", "seq", None, None, None),
            P("grp", None, None, "seq"),
            P("grp", None, None, "seq"),
        ),
        check_vma=False,
    )
```

```python
import functools

import jax
import jax.numpy as jnp
import numpy as np
from jax import lax
from jax.experimental import pallas as pl
from jax.experimental.pallas import tpu as pltpu
from jax.sharding import PartitionSpec as P

NSTATE = 16
KCONV = 4
BLOCK = 16
MOST = 3
LANES = 128
RIM = 8
STEPS = 8
LOG2E = 1.4426950408889634
LOG2LOG2E = 0.5287663729448977
MSG = 24
VMEM_BYTES = 62 * 1024 * 1024
WIDE_BYTES = 48 * 1024 * 1024
SMALL_BYTES = 16 * 1024 * 1024
F32 = jnp.float32
BF16 = jnp.bfloat16

VM = functools.partial(pl.BlockSpec, memory_space=pltpu.VMEM)
SM = pl.BlockSpec(memory_space=pltpu.SMEM)


def silu_of_half(h):
    return h + h * jnp.tanh(h)


def rate_of(log):
    return jnp.exp2(log * LOG2E + LOG2LOG2E)


def split(v):
    high = v.astype(BF16)
    return high, (v - high.astype(F32)).astype(BF16)


def segment_end(count_ref, length):
    return count_ref[lax.axis_index("grp")] * BLOCK - lax.axis_index("seq") * length


def prepare_kernel(
    width, count_ref, step_ref, sbias_ref, proj_ref, dt_ref, b_ref, c_ref
):
    length, channels = step_ref.shape
    groups = length // NSTATE
    seg_end = segment_end(count_ref, length)

    @pl.when(pl.program_id(0) == 0)
    def _():
        b_rows = proj_ref[0].astype(F32)
        for t in range(length):
            b_ref[t] = jnp.broadcast_to(-b_rows[:, t : t + 1], (NSTATE, LANES))
        wide = NSTATE * NSTATE
        spread = lax.broadcasted_iota(jnp.int32, (NSTATE, wide), 1) % NSTATE
        spread = (spread == lax.broadcasted_iota(jnp.int32, (NSTATE, wide), 0)).astype(BF16)
        tiled = lax.dot_general(
            proj_ref[1], spread, (((0,), (0,)), ((), ())), preferred_element_type=F32
        )
        row = lax.broadcasted_iota(jnp.int32, (length, wide), 0) % NSTATE
        col = lax.broadcasted_iota(jnp.int32, (length, wide), 1) // NSTATE
        c_ref[...] = jnp.where(row == col, tiled, 0.0).astype(BF16).reshape(groups, NSTATE, wide)

    live = lax.broadcasted_iota(jnp.int32, (length, width), 0) < seg_end
    for lane in range(0, channels, width):
        cut = pl.ds(lane, width)
        e = jnp.exp2(step_ref[:, cut].astype(F32) * LOG2E + sbias_ref[:, cut] * LOG2E)
        minus_dt = jnp.where(e < 2e-3, e * (0.5 * e - 1.0), -jnp.log(1.0 + e))
        minus_dt = jnp.where(live, minus_dt, 0.0)
        dt_ref[:, :, cut] = minus_dt.reshape(groups, NSTATE, width)


def prepare(count, step, sbias, proj, steps, width=512):
    length, channels = step.shape
    groups = length // NSTATE
    piece = channels // steps
    blocks = pl.BlockSpec((groups, NSTATE, piece), lambda j: (0, 0, j))
    whole = lambda shape: pl.BlockSpec(shape, lambda j: (0,) * len(shape))
    b_shape = (length, NSTATE, LANES)
    c_shape = (groups, NSTATE, NSTATE * NSTATE)
    return pl.pallas_call(
        functools.partial(prepare_kernel, width),
        grid=(steps,),
        in_specs=[
            SM,
            pl.BlockSpec((length, piece), lambda j: (0, j)),
            pl.BlockSpec((1, piece), lambda j: (0, j)),
            whole(proj.shape),
        ],
        out_specs=[blocks, whole(b_shape), whole(c_shape)],
        out_shape=[
            jax.ShapeDtypeStruct((groups, NSTATE, channels), F32),
            jax.ShapeDtypeStruct(b_shape, F32),
            jax.ShapeDtypeStruct(c_shape, BF16),
        ],
        compiler_params=pltpu.CompilerParams(vmem_limit_bytes=VMEM_BYTES),
        cost_estimate=pl.CostEstimate(
            flops=20 * length * channels,
            bytes_accessed=10 * length * channels,
            transcendentals=2 * length * channels,
        ),
        name="prepare",
    )(count, step, sbias, proj)


def scan_kernel(
    width,
    count_ref,
    x_ref,
    halo_ref,
    dt_ref,
    log_ref,
    cw_ref,
    cbias_ref,
    skip_ref,
    b_ref,
    c_ref,
    shift_ref,
    tri_ref,
    out_ref,
    run_ref,
    msg_ref,
    drive_s,
    rate_s,
):
    length, channels = x_ref.shape
    groups = length // NSTATE
    seg_end = segment_end(count_ref, length)
    held = jnp.logical_and(seg_end >= 1, seg_end <= length).astype(F32)
    tail_at = pl.multiple_of(jnp.clip(seg_end - NSTATE, 0, length - NSTATE), NSTATE)

    base = pl.program_id(0) * channels
    piece = msg_ref.shape[2]

    def tile(l, carry):
        cut = pl.ds(pl.multiple_of(l * width, width), width)
        at = pl.ds(pl.multiple_of(base + l * width, width), width)
        x = x_ref[:, cut]
        moved = jnp.dot(
            shift_ref[...],
            jnp.concatenate([x, halo_ref[:, at]], axis=0),
            preferred_element_type=F32,
        )
        half_w = 0.5 * cw_ref[:, at]
        half = 0.5 * cbias_ref[:, at] + half_w[KCONV - 1 :] * x.astype(F32)
        for k in range(KCONV - 1):
            half = half + half_w[k : k + 1] * moved[k * length : (k + 1) * length]
        driven = silu_of_half(half).reshape(groups, NSTATE, width)
        dt = dt_ref[:, :, cut]
        drive_s[...] = dt * driven
        high, low = split(dt.reshape(length, width))
        run = jnp.dot(
            tri_ref[...], jnp.concatenate([high, low], axis=0), preferred_element_type=F32
        )
        run_ref[:, :, cut] = run.reshape(groups, NSTATE, width)
        out_ref[:, :, cut] = skip_ref[:, at] * driven
        rate_s[...] = rate_of(log_ref[:, at])

        def one_group(i, state):
            rates = rate_s[...]
            mixes = []
            for tt in range(NSTATE):
                dt_now = dt_ref[i, pl.ds(tt, 1), cut]
                drive_now = drive_s[i, pl.ds(tt, 1), :]
                b_now = jnp.concatenate([b_ref[i * NSTATE + tt]] * (width // LANES), axis=1)
                state = jnp.exp2(dt_now * rates) * state + drive_now * b_now
                mixes.append(state.astype(BF16))
            out_ref[i, :, cut] += jnp.dot(
                c_ref[i], jnp.concatenate(mixes, axis=0), preferred_element_type=F32
            )
            return state

        state = lax.fori_loop(0, groups, one_group, jnp.zeros((NSTATE, width), F32), unroll=True)
        s_high, s_low = split(run[length - 1 :])
        tail = x_ref[pl.ds(tail_at, NSTATE), cut].astype(F32) * held
        message = jnp.concatenate(
            [
                state,
                s_high.astype(F32),
                s_low.astype(F32),
                tail[NSTATE - (KCONV - 1) :],
                jnp.zeros((MSG - NSTATE - 2 - (KCONV - 1), width), F32),
            ],
            axis=0,
        )
        inside = pl.ds(pl.multiple_of((l * width) % piece, width), width)
        msg_ref[(l * width) // piece, :, inside] = message.astype(BF16)
        return carry

    lax.fori_loop(0, channels // width, tile, 0)


def local_scan(
    count, x, halo, dt, log, cw, cbias, skip, b_wide, c_diag, pieces, steps, width=512
):
    length, channels = x.shape
    groups = length // NSTATE
    piece = channels // pieces
    block = channels // steps
    rim = halo.shape[0]
    shift = np.zeros(((KCONV - 1) * length, length + rim), np.float32)
    for k in range(KCONV - 1):
        for t in range(length):
            source = t - (KCONV - 1) + k
            shift[k * length + t, source if source >= 0 else length + rim + source] = 1.0
    shift = jnp.asarray(shift, BF16)
    tri = np.tril(np.ones((length, length), np.float32))
    tri = jnp.asarray(np.concatenate([tri, tri], axis=1), BF16)
    per = lambda rows: pl.BlockSpec((rows, block), lambda j: (0, j))
    blocks = pl.BlockSpec((groups, NSTATE, block), lambda j: (0, 0, j))
    whole = lambda a: pl.BlockSpec(a.shape, lambda j: (0,) * a.ndim)
    return pl.pallas_call(
        functools.partial(scan_kernel, width),
        grid=(steps,),
        in_specs=[
            SM,
            per(length),
            VM(),
            blocks,
            whole(log),
            whole(cw),
            whole(cbias),
            whole(skip),
            whole(b_wide),
            whole(c_diag),
            whole(shift),
            whole(tri),
        ],
        out_specs=[blocks, blocks, pl.BlockSpec((block // piece, MSG, piece), lambda j: (j, 0, 0))],
        out_shape=[
            jax.ShapeDtypeStruct((groups, NSTATE, channels), F32),
            jax.ShapeDtypeStruct((groups, NSTATE, channels), F32),
            jax.ShapeDtypeStruct((pieces, MSG, piece), BF16),
        ],
        scratch_shapes=[
            pltpu.VMEM((groups, NSTATE, width), F32),
            pltpu.VMEM((NSTATE, width), F32),
        ],
        compiler_params=pltpu.CompilerParams(vmem_limit_bytes=VMEM_BYTES),
        cost_estimate=pl.CostEstimate(
            flops=8 * length * channels * NSTATE,
            bytes_accessed=12 * length * channels,
            transcendentals=length * channels * NSTATE,
        ),
        name="local_scan",
    )(count, x, halo, dt, log, cw, cbias, skip, b_wide, c_diag, shift, tri)


def chain_kernel(dest_ref, got_ref, log_ref, start_ref, final_ref):
    pieces, _, piece = got_ref.shape
    own = pl.ds(pl.multiple_of(lax.axis_index("seq") * piece, piece), piece)
    rates = rate_of(log_ref[:, own])
    state = jnp.zeros((NSTATE, piece), F32)
    tails = jnp.zeros((MSG - NSTATE, piece), F32)
    for r in range(pieces):
        start_ref[r] = state.astype(BF16)
        got = got_ref[r].astype(F32)
        total = got[NSTATE : NSTATE + 1] + got[NSTATE + 1 : NSTATE + 2]
        state = jnp.exp2(total * rates) * state + got[:NSTATE]
        tails = tails + got[NSTATE:]
    final_ref[...] = jnp.zeros_like(final_ref)
    dest = dest_ref[lax.axis_index("grp")]
    final_ref[dest] = jnp.concatenate([state, tails], axis=0).astype(BF16)


def chain(decode_device, got, log, groups):
    pieces, _, piece = got.shape
    return pl.pallas_call(
        chain_kernel,
        in_specs=[SM, VM(), VM()],
        out_specs=[VM(), VM()],
        out_shape=[
            jax.ShapeDtypeStruct((pieces, NSTATE, piece), BF16),
            jax.ShapeDtypeStruct((groups, MSG, piece), BF16),
        ],
        compiler_params=pltpu.CompilerParams(vmem_limit_bytes=SMALL_BYTES),
        name="chain",
    )(decode_device, got, log)


def finish_kernel(
    width, count_ref, start_ref, out_ref, run_ref, log_ref, gate_ref, c_ref, mixed_ref, rate_s, start_s
):
    length, channels = gate_ref.shape
    groups = length // NSTATE
    seg_end = segment_end(count_ref, length)
    base = pl.program_id(0) * channels
    piece = start_ref.shape[2]

    def tile(l, carry):
        cut = pl.ds(pl.multiple_of(l * width, width), width)
        at = pl.ds(pl.multiple_of(base + l * width, width), width)
        inside = pl.ds(pl.multiple_of((l * width) % piece, width), width)
        rate_s[...] = rate_of(log_ref[:, at]).astype(BF16)
        start_s[...] = start_ref[(l * width) // piece, :, inside]

        def one_group(i, carry):
            rates, start = rate_s[...], start_s[...]
            mixes = []
            for tt in range(NSTATE):
                run_now = jnp.broadcast_to(run_ref[i, pl.ds(tt, 1), cut], (NSTATE, width))
                mixes.append(jnp.exp2(run_now.astype(BF16) * rates) * start)
            carried = jnp.dot(
                c_ref[i], jnp.concatenate(mixes, axis=0), preferred_element_type=F32
            )
            rows = pl.ds(pl.multiple_of(i * NSTATE, NSTATE), NSTATE)
            gate = silu_of_half(0.5 * gate_ref[rows, cut].astype(F32))
            mixed = (out_ref[i, :, cut] + carried) * gate
            row = lax.broadcasted_iota(jnp.int32, (NSTATE, width), 0) + i * NSTATE
            mixed_ref[rows, cut] = jnp.where(row < seg_end, mixed, 0.0).astype(BF16)
            return carry

        lax.fori_loop(0, groups, one_group, 0, unroll=True)
        return carry

    lax.fori_loop(0, channels // width, tile, 0)


def finish(count, start, out, run, log, gate, c_diag, steps, width=1024):
    length, channels = gate.shape
    groups = length // NSTATE
    pieces, _, piece = start.shape
    block = channels // steps
    per = lambda rows: pl.BlockSpec((rows, block), lambda j: (0, j))
    blocks = pl.BlockSpec((groups, NSTATE, block), lambda j: (0, 0, j))
    return pl.pallas_call(
        functools.partial(finish_kernel, width),
        grid=(steps,),
        in_specs=[
            SM,
            pl.BlockSpec((block // piece, NSTATE, piece), lambda j: (j, 0, 0)),
            blocks,
            blocks,
            pl.BlockSpec(log.shape, lambda j: (0, 0)),
            per(length),
            pl.BlockSpec(c_diag.shape, lambda j: (0, 0, 0)),
        ],
        out_specs=per(length),
        out_shape=jax.ShapeDtypeStruct((length, channels), BF16),
        scratch_shapes=[pltpu.VMEM((NSTATE, width), BF16), pltpu.VMEM((NSTATE, width), BF16)],
        compiler_params=pltpu.CompilerParams(vmem_limit_bytes=VMEM_BYTES),
        cost_estimate=pl.CostEstimate(
            flops=4 * length * channels * NSTATE,
            bytes_accessed=12 * length * channels,
            transcendentals=length * channels * NSTATE,
        ),
        name="finish",
    )(count, start, out, run, log, gate, c_diag)


def caches_kernel(
    here,
    dest_ref,
    count_ref,
    slot_ref,
    kv_ref,
    got_ref,
    cache_ref,
    state_ref,
    rows_ref,
    kv_s,
    zero_s,
    used_s,
    in_sems,
    out_sems,
):
    groups, capacity = got_ref.shape[0], cache_ref.shape[0]
    grp_pos = lax.axis_index("grp")
    first = lax.axis_index("seq") * here

    def clear(c, carry):
        used_s[c] = 0
        return carry

    lax.fori_loop(0, capacity, clear, 0)

    def each_block(act):
        def request(g, carry):
            @pl.when(dest_ref[g] == grp_pos)
            def _():
                def block(j, carry):
                    act(g, j, slot_ref[g, first + j])
                    return carry

                lax.fori_loop(0, jnp.clip(count_ref[g] - first, 0, here), block, 0)

            return carry

        lax.fori_loop(0, groups, request, 0)

    def into(g, j, slot):
        return pltpu.make_async_copy(kv_ref.at[g, j], kv_s.at[slot], in_sems.at[slot])

    def out_of(source, slot):
        return pltpu.make_async_copy(source, cache_ref.at[slot], out_sems.at[slot])

    def fetch(g, j, slot):
        used_s[slot] = 1
        into(g, j, slot).start()

    each_block(fetch)
    zero_s[...] = jnp.zeros_like(zero_s)

    def fill(c, carry):
        @pl.when(used_s[c] == 0)
        def _():
            out_of(zero_s, c).start()

        return carry

    lax.fori_loop(0, capacity, fill, 0)
    state_ref[...] = jnp.zeros_like(state_ref)
    rows_ref[...] = jnp.zeros_like(rows_ref)

    def one(g, taken):
        mine = dest_ref[g] == grp_pos

        @pl.when(mine)
        def _():
            got = got_ref[g].astype(F32)
            state_ref[taken] = got[:NSTATE]
            rows_ref[taken] = got[NSTATE + 2 : NSTATE + 1 + KCONV].astype(BF16)

        return taken + mine.astype(jnp.int32)

    lax.fori_loop(0, groups, one, jnp.int32(0))

    def forward(g, j, slot):
        into(g, j, slot).wait()
        out_of(kv_s.at[slot], slot).start()

    each_block(forward)

    def ended(c, carry):
        out_of(zero_s, c).wait()
        return carry

    lax.fori_loop(0, capacity, ended, 0)


def caches(decode_device, block_count, block_slot, kv, got, here, capacity):
    piece = got.shape[2]
    width = kv.shape[-1]
    return pl.pallas_call(
        functools.partial(caches_kernel, here),
        in_specs=[
            SM,
            SM,
            SM,
            pl.BlockSpec(memory_space=pl.ANY),
            VM(),
        ],
        out_specs=[pl.BlockSpec(memory_space=pl.ANY), VM(), VM()],
        out_shape=[
            jax.ShapeDtypeStruct((capacity, BLOCK, width), BF16),
            jax.ShapeDtypeStruct((MOST, NSTATE, piece), F32),
            jax.ShapeDtypeStruct((MOST, KCONV - 1, piece), BF16),
        ],
        scratch_shapes=[
            pltpu.VMEM((capacity, BLOCK, width), BF16),
            pltpu.VMEM((BLOCK, width), BF16),
            pltpu.SMEM((capacity,), jnp.int32),
            pltpu.SemaphoreType.DMA((capacity,)),
            pltpu.SemaphoreType.DMA((capacity,)),
        ],
        compiler_params=pltpu.CompilerParams(vmem_limit_bytes=WIDE_BYTES),
        name="caches",
    )(decode_device, block_count, block_slot, kv, got)


def per_device(
    mamba_input,
    gate_input,
    step_raw,
    scan_proj,
    decay_log,
    step_bias,
    conv_weight,
    conv_bias,
    skip_gain,
    kv_rows,
    decode_device,
    block_count,
    block_slot,
):
    seg_len, channels = mamba_input.shape[1:]
    groups = lax.axis_size("grp")
    pieces = lax.axis_size("seq")
    here = seg_len // BLOCK
    x = mamba_input[0]

    kv_all = lax.all_gather(kv_rows[0].reshape(here, BLOCK, kv_rows.shape[2]), "grp")
    halo = lax.ppermute(x[seg_len - RIM :], "seq", [(s, s + 1) for s in range(pieces - 1)])
    dt, b_wide, c_diag = prepare(block_count, step_raw[0], step_bias[None], scan_proj[0], 2)
    out, run, msg = local_scan(
        block_count,
        x,
        halo,
        dt,
        decay_log,
        conv_weight,
        conv_bias[None],
        skip_gain[None],
        b_wide,
        c_diag,
        pieces,
        STEPS,
    )
    got = lax.all_to_all(msg, "seq", split_axis=0, concat_axis=0, tiled=True)
    starts, final = chain(decode_device, got, decay_log, groups)
    start = lax.all_to_all(starts, "seq", split_axis=0, concat_axis=0, tiled=True)
    final_got = lax.all_to_all(final, "grp", split_axis=0, concat_axis=0, tiled=True)
    block_out = finish(block_count, start, out, run, decay_log, gate_input[0], c_diag, STEPS)
    kv_cache, ssm_cache, conv_cache = caches(
        decode_device, block_count, block_slot, kv_all, final_got, here, MOST * here
    )
    return block_out[None], kv_cache[None, None], ssm_cache[None], conv_cache[None]


def solution(mesh):
    return jax.shard_map(
        per_device,
        mesh=mesh,
        in_specs=(
            P("grp", "seq", None),
            P("grp", "seq", None),
            P("grp", "seq", None),
            P("grp", None, None, "seq"),
            P(),
            P(),
            P(),
            P(),
            P(),
            P("grp", "seq", None),
            P(),
            P(),
            P(),
        ),
        out_specs=(
            P("grp", "seq", None),
            P("grp", "seq", None, None, None),
            P("grp", None, None, "seq"),
            P("grp", None, None, "seq"),
        ),
        check_vma=False,
    )
```

```python
import functools

import jax
import jax.numpy as jnp
import numpy as np
from jax import lax
from jax.experimental import pallas as pl
from jax.experimental.pallas import tpu as pltpu
from jax.sharding import PartitionSpec as P

NSTATE = 16
KCONV = 4
BLOCK = 16
MOST = 3
LANES = 128
RIM = 8
STEPS = 8
LOG2E = 1.4426950408889634
LOG2LOG2E = 0.5287663729448977
MSG = 24
VMEM_BYTES = 62 * 1024 * 1024
WIDE_BYTES = 48 * 1024 * 1024
SMALL_BYTES = 16 * 1024 * 1024
F32 = jnp.float32
BF16 = jnp.bfloat16

VM = functools.partial(pl.BlockSpec, memory_space=pltpu.VMEM)
SM = pl.BlockSpec(memory_space=pltpu.SMEM)


def silu_of_half(h):
    return h + h * jnp.tanh(h)


def rate_of(log):
    return jnp.exp2(log * LOG2E + LOG2LOG2E)


def split(v):
    high = v.astype(BF16)
    return high, (v - high.astype(F32)).astype(BF16)


def segment_end(count_ref, length):
    return count_ref[lax.axis_index("grp")] * BLOCK - lax.axis_index("seq") * length


def prepare_kernel(
    width, count_ref, step_ref, sbias_ref, proj_ref, dt_ref, b_ref, c_ref
):
    length, channels = step_ref.shape
    groups = length // NSTATE
    seg_end = segment_end(count_ref, length)

    @pl.when(pl.program_id(0) == 0)
    def _():
        b_rows = proj_ref[0].astype(F32)
        for t in range(length):
            b_ref[t] = jnp.broadcast_to(-b_rows[:, t : t + 1], (NSTATE, LANES))
        wide = NSTATE * NSTATE
        spread = lax.broadcasted_iota(jnp.int32, (NSTATE, wide), 1) % NSTATE
        spread = (spread == lax.broadcasted_iota(jnp.int32, (NSTATE, wide), 0)).astype(BF16)
        tiled = lax.dot_general(
            proj_ref[1], spread, (((0,), (0,)), ((), ())), preferred_element_type=F32
        )
        row = lax.broadcasted_iota(jnp.int32, (length, wide), 0) % NSTATE
        col = lax.broadcasted_iota(jnp.int32, (length, wide), 1) // NSTATE
        c_ref[...] = jnp.where(row == col, tiled, 0.0).astype(BF16).reshape(groups, NSTATE, wide)

    live = lax.broadcasted_iota(jnp.int32, (length, width), 0) < seg_end
    for lane in range(0, channels, width):
        cut = pl.ds(lane, width)
        e = jnp.exp2(step_ref[:, cut].astype(F32) * LOG2E + sbias_ref[:, cut] * LOG2E)
        minus_dt = jnp.where(e < 2e-3, e * (0.5 * e - 1.0), -jnp.log(1.0 + e))
        minus_dt = jnp.where(live, minus_dt, 0.0)
        dt_ref[:, :, cut] = minus_dt.reshape(groups, NSTATE, width)


def prepare(count, step, sbias, proj, steps, width=512):
    length, channels = step.shape
    groups = length // NSTATE
    piece = channels // steps
    blocks = pl.BlockSpec((groups, NSTATE, piece), lambda j: (0, 0, j))
    whole = lambda shape: pl.BlockSpec(shape, lambda j: (0,) * len(shape))
    b_shape = (length, NSTATE, LANES)
    c_shape = (groups, NSTATE, NSTATE * NSTATE)
    return pl.pallas_call(
        functools.partial(prepare_kernel, width),
        grid=(steps,),
        in_specs=[
            SM,
            pl.BlockSpec((length, piece), lambda j: (0, j)),
            pl.BlockSpec((1, piece), lambda j: (0, j)),
            whole(proj.shape),
        ],
        out_specs=[blocks, whole(b_shape), whole(c_shape)],
        out_shape=[
            jax.ShapeDtypeStruct((groups, NSTATE, channels), F32),
            jax.ShapeDtypeStruct(b_shape, F32),
            jax.ShapeDtypeStruct(c_shape, BF16),
        ],
        compiler_params=pltpu.CompilerParams(vmem_limit_bytes=VMEM_BYTES),
        cost_estimate=pl.CostEstimate(
            flops=20 * length * channels,
            bytes_accessed=10 * length * channels,
            transcendentals=2 * length * channels,
        ),
        name="prepare",
    )(count, step, sbias, proj)


def scan_kernel(
    width,
    count_ref,
    x_ref,
    halo_ref,
    dt_ref,
    log_ref,
    cw_ref,
    cbias_ref,
    skip_ref,
    b_ref,
    c_ref,
    shift_ref,
    tri_ref,
    out_ref,
    run_ref,
    msg_ref,
    drive_s,
    rate_s,
):
    length, channels = x_ref.shape
    groups = length // NSTATE
    seg_end = segment_end(count_ref, length)
    held = jnp.logical_and(seg_end >= 1, seg_end <= length).astype(F32)
    tail_at = pl.multiple_of(jnp.clip(seg_end - NSTATE, 0, length - NSTATE), NSTATE)

    base = pl.program_id(0) * channels
    piece = msg_ref.shape[2]

    def tile(l, carry):
        cut = pl.ds(pl.multiple_of(l * width, width), width)
        at = pl.ds(pl.multiple_of(base + l * width, width), width)
        x = x_ref[:, cut]
        moved = jnp.dot(
            shift_ref[...],
            jnp.concatenate([x, halo_ref[:, at]], axis=0),
            preferred_element_type=F32,
        )
        half_w = 0.5 * cw_ref[:, at]
        half = 0.5 * cbias_ref[:, at] + half_w[KCONV - 1 :] * x.astype(F32)
        for k in range(KCONV - 1):
            half = half + half_w[k : k + 1] * moved[k * length : (k + 1) * length]
        driven = silu_of_half(half).reshape(groups, NSTATE, width)
        dt = dt_ref[:, :, cut]
        drive_s[...] = dt * driven
        high, low = split(dt.reshape(length, width))
        run = jnp.dot(
            tri_ref[...], jnp.concatenate([high, low], axis=0), preferred_element_type=F32
        )
        run_ref[:, :, cut] = run.reshape(groups, NSTATE, width)
        out_ref[:, :, cut] = skip_ref[:, at] * driven
        rate_s[...] = rate_of(log_ref[:, at])

        def one_group(i, state):
            rates = rate_s[...]
            mixes = []
            for tt in range(NSTATE):
                dt_now = dt_ref[i, pl.ds(tt, 1), cut]
                drive_now = drive_s[i, pl.ds(tt, 1), :]
                b_now = jnp.concatenate([b_ref[i * NSTATE + tt]] * (width // LANES), axis=1)
                state = jnp.exp2(dt_now * rates) * state + drive_now * b_now
                mixes.append(state.astype(BF16))
            out_ref[i, :, cut] += jnp.dot(
                c_ref[i], jnp.concatenate(mixes, axis=0), preferred_element_type=F32
            )
            return state

        state = lax.fori_loop(0, groups, one_group, jnp.zeros((NSTATE, width), F32), unroll=True)
        s_high, s_low = split(run[length - 1 :])
        tail = x_ref[pl.ds(tail_at, NSTATE), cut].astype(F32) * held
        message = jnp.concatenate(
            [
                state,
                s_high.astype(F32),
                s_low.astype(F32),
                tail[NSTATE - (KCONV - 1) :],
                jnp.zeros((MSG - NSTATE - 2 - (KCONV - 1), width), F32),
            ],
            axis=0,
        )
        inside = pl.ds(pl.multiple_of((l * width) % piece, width), width)
        msg_ref[(l * width) // piece, :, inside] = message.astype(BF16)
        return carry

    lax.fori_loop(0, channels // width, tile, 0, unroll=True)


def local_scan(
    count, x, halo, dt, log, cw, cbias, skip, b_wide, c_diag, pieces, steps, width=512
):
    length, channels = x.shape
    groups = length // NSTATE
    piece = channels // pieces
    block = channels // steps
    rim = halo.shape[0]
    shift = np.zeros(((KCONV - 1) * length, length + rim), np.float32)
    for k in range(KCONV - 1):
        for t in range(length):
            source = t - (KCONV - 1) + k
            shift[k * length + t, source if source >= 0 else length + rim + source] = 1.0
    shift = jnp.asarray(shift, BF16)
    tri = np.tril(np.ones((length, length), np.float32))
    tri = jnp.asarray(np.concatenate([tri, tri], axis=1), BF16)
    per = lambda rows: pl.BlockSpec((rows, block), lambda j: (0, j))
    blocks = pl.BlockSpec((groups, NSTATE, block), lambda j: (0, 0, j))
    whole = lambda a: pl.BlockSpec(a.shape, lambda j: (0,) * a.ndim)
    return pl.pallas_call(
        functools.partial(scan_kernel, width),
        grid=(steps,),
        in_specs=[
            SM,
            per(length),
            whole(halo),
            blocks,
            whole(log),
            whole(cw),
            whole(cbias),
            whole(skip),
            whole(b_wide),
            whole(c_diag),
            whole(shift),
            whole(tri),
        ],
        out_specs=[blocks, blocks, pl.BlockSpec((block // piece, MSG, piece), lambda j: (j, 0, 0))],
        out_shape=[
            jax.ShapeDtypeStruct((groups, NSTATE, channels), F32),
            jax.ShapeDtypeStruct((groups, NSTATE, channels), F32),
            jax.ShapeDtypeStruct((pieces, MSG, piece), BF16),
        ],
        scratch_shapes=[
            pltpu.VMEM((groups, NSTATE, width), F32),
            pltpu.VMEM((NSTATE, width), F32),
        ],
        compiler_params=pltpu.CompilerParams(vmem_limit_bytes=VMEM_BYTES),
        cost_estimate=pl.CostEstimate(
            flops=8 * length * channels * NSTATE,
            bytes_accessed=12 * length * channels,
            transcendentals=length * channels * NSTATE,
        ),
        name="local_scan",
    )(count, x, halo, dt, log, cw, cbias, skip, b_wide, c_diag, shift, tri)


def chain_kernel(dest_ref, got_ref, log_ref, start_ref, final_ref):
    pieces, _, piece = got_ref.shape
    own = pl.ds(pl.multiple_of(lax.axis_index("seq") * piece, piece), piece)
    rates = rate_of(log_ref[:, own])
    state = jnp.zeros((NSTATE, piece), F32)
    tails = jnp.zeros((MSG - NSTATE, piece), F32)
    for r in range(pieces):
        start_ref[r] = state.astype(BF16)
        got = got_ref[r].astype(F32)
        total = got[NSTATE : NSTATE + 1] + got[NSTATE + 1 : NSTATE + 2]
        state = jnp.exp2(total * rates) * state + got[:NSTATE]
        tails = tails + got[NSTATE:]
    final_ref[...] = jnp.zeros_like(final_ref)
    dest = dest_ref[lax.axis_index("grp")]
    final_ref[dest] = jnp.concatenate([state, tails], axis=0).astype(BF16)


def chain(decode_device, got, log, groups):
    pieces, _, piece = got.shape
    return pl.pallas_call(
        chain_kernel,
        in_specs=[SM, VM(), VM()],
        out_specs=[VM(), VM()],
        out_shape=[
            jax.ShapeDtypeStruct((pieces, NSTATE, piece), BF16),
            jax.ShapeDtypeStruct((groups, MSG, piece), BF16),
        ],
        compiler_params=pltpu.CompilerParams(vmem_limit_bytes=SMALL_BYTES),
        name="chain",
    )(decode_device, got, log)


def finish_kernel(
    width, count_ref, start_ref, out_ref, run_ref, log_ref, gate_ref, c_ref, mixed_ref, rate_s, start_s
):
    length, channels = gate_ref.shape
    groups = length // NSTATE
    seg_end = segment_end(count_ref, length)
    base = pl.program_id(0) * channels
    piece = start_ref.shape[2]

    def tile(l, carry):
        cut = pl.ds(pl.multiple_of(l * width, width), width)
        at = pl.ds(pl.multiple_of(base + l * width, width), width)
        inside = pl.ds(pl.multiple_of((l * width) % piece, width), width)
        rate_s[...] = rate_of(log_ref[:, at]).astype(BF16)
        start_s[...] = start_ref[(l * width) // piece, :, inside]

        def one_group(i, carry):
            rates, start = rate_s[...], start_s[...]
            mixes = []
            for tt in range(NSTATE):
                run_now = jnp.broadcast_to(run_ref[i, pl.ds(tt, 1), cut], (NSTATE, width))
                mixes.append(jnp.exp2(run_now.astype(BF16) * rates) * start)
            carried = jnp.dot(
                c_ref[i], jnp.concatenate(mixes, axis=0), preferred_element_type=F32
            )
            rows = pl.ds(pl.multiple_of(i * NSTATE, NSTATE), NSTATE)
            gate = silu_of_half(0.5 * gate_ref[rows, cut].astype(F32))
            mixed = (out_ref[i, :, cut] + carried) * gate
            row = lax.broadcasted_iota(jnp.int32, (NSTATE, width), 0) + i * NSTATE
            mixed_ref[rows, cut] = jnp.where(row < seg_end, mixed, 0.0).astype(BF16)
            return carry

        lax.fori_loop(0, groups, one_group, 0, unroll=True)
        return carry

    lax.fori_loop(0, channels // width, tile, 0)


def finish(count, start, out, run, log, gate, c_diag, steps, width=1024):
    length, channels = gate.shape
    groups = length // NSTATE
    pieces, _, piece = start.shape
    block = channels // steps
    per = lambda rows: pl.BlockSpec((rows, block), lambda j: (0, j))
    blocks = pl.BlockSpec((groups, NSTATE, block), lambda j: (0, 0, j))
    return pl.pallas_call(
        functools.partial(finish_kernel, width),
        grid=(steps,),
        in_specs=[
            SM,
            pl.BlockSpec((block // piece, NSTATE, piece), lambda j: (j, 0, 0)),
            blocks,
            blocks,
            pl.BlockSpec(log.shape, lambda j: (0, 0)),
            per(length),
            pl.BlockSpec(c_diag.shape, lambda j: (0, 0, 0)),
        ],
        out_specs=per(length),
        out_shape=jax.ShapeDtypeStruct((length, channels), BF16),
        scratch_shapes=[pltpu.VMEM((NSTATE, width), BF16), pltpu.VMEM((NSTATE, width), BF16)],
        compiler_params=pltpu.CompilerParams(vmem_limit_bytes=VMEM_BYTES),
        cost_estimate=pl.CostEstimate(
            flops=4 * length * channels * NSTATE,
            bytes_accessed=12 * length * channels,
            transcendentals=length * channels * NSTATE,
        ),
        name="finish",
    )(count, start, out, run, log, gate, c_diag)


def caches_kernel(
    here,
    dest_ref,
    count_ref,
    slot_ref,
    kv_ref,
    got_ref,
    cache_ref,
    state_ref,
    rows_ref,
    zero_s,
    used_s,
    sem,
):
    groups, capacity = got_ref.shape[0], cache_ref.shape[0]
    grp_pos = lax.axis_index("grp")
    first = lax.axis_index("seq") * here
    for c in range(capacity):
        used_s[c] = 0

    def request(g, carry):
        @pl.when(dest_ref[g] == grp_pos)
        def _():
            last = count_ref[g] - first
            for j in range(here):

                @pl.when(j < last)
                def _():
                    slot = slot_ref[g, first + j]
                    used_s[slot] = 1
                    pltpu.make_async_copy(kv_ref.at[g, j], cache_ref.at[slot], sem).start()

        return carry

    lax.fori_loop(0, groups, request, 0)
    zero_s[...] = jnp.zeros_like(zero_s)
    for c in range(capacity):

        @pl.when(used_s[c] == 0)
        def _():
            pltpu.make_async_copy(zero_s, cache_ref.at[c], sem).start()

    state_ref[...] = jnp.zeros_like(state_ref)
    rows_ref[...] = jnp.zeros_like(rows_ref)

    def one(g, taken):
        mine = dest_ref[g] == grp_pos

        @pl.when(mine)
        def _():
            got = got_ref[g].astype(F32)
            state_ref[taken] = got[:NSTATE]
            rows_ref[taken] = got[NSTATE + 2 : NSTATE + 1 + KCONV].astype(BF16)

        return taken + mine.astype(jnp.int32)

    lax.fori_loop(0, groups, one, jnp.int32(0))
    pltpu.make_async_copy(cache_ref, cache_ref, sem).wait()


def caches(decode_device, block_count, block_slot, kv, got, here, capacity):
    piece = got.shape[2]
    width = kv.shape[-1]
    return pl.pallas_call(
        functools.partial(caches_kernel, here),
        in_specs=[
            SM,
            SM,
            SM,
            pl.BlockSpec(memory_space=pl.ANY),
            VM(),
        ],
        out_specs=[VM(), VM(), VM()],
        out_shape=[
            jax.ShapeDtypeStruct((capacity, BLOCK, width), BF16),
            jax.ShapeDtypeStruct((MOST, NSTATE, piece), F32),
            jax.ShapeDtypeStruct((MOST, KCONV - 1, piece), BF16),
        ],
        scratch_shapes=[
            pltpu.VMEM((BLOCK, width), BF16),
            pltpu.SMEM((capacity,), jnp.int32),
            pltpu.SemaphoreType.DMA,
        ],
        compiler_params=pltpu.CompilerParams(vmem_limit_bytes=WIDE_BYTES),
        name="caches",
    )(decode_device, block_count, block_slot, kv, got)


def per_device(
    mamba_input,
    gate_input,
    step_raw,
    scan_proj,
    decay_log,
    step_bias,
    conv_weight,
    conv_bias,
    skip_gain,
    kv_rows,
    decode_device,
    block_count,
    block_slot,
):
    seg_len, channels = mamba_input.shape[1:]
    groups = lax.axis_size("grp")
    pieces = lax.axis_size("seq")
    here = seg_len // BLOCK
    x = mamba_input[0]

    kv_all = lax.all_gather(kv_rows[0].reshape(here, BLOCK, kv_rows.shape[2]), "grp")
    halo = lax.ppermute(x[seg_len - RIM :], "seq", [(s, s + 1) for s in range(pieces - 1)])
    dt, b_wide, c_diag = prepare(block_count, step_raw[0], step_bias[None], scan_proj[0], 2)
    out, run, msg = local_scan(
        block_count,
        x,
        halo,
        dt,
        decay_log,
        conv_weight,
        conv_bias[None],
        skip_gain[None],
        b_wide,
        c_diag,
        pieces,
        STEPS,
    )
    got = lax.all_to_all(msg, "seq", split_axis=0, concat_axis=0, tiled=True)
    starts, final = chain(decode_device, got, decay_log, groups)
    start = lax.all_to_all(starts, "seq", split_axis=0, concat_axis=0, tiled=True)
    final_got = lax.all_to_all(final, "grp", split_axis=0, concat_axis=0, tiled=True)
    block_out = finish(block_count, start, out, run, decay_log, gate_input[0], c_diag, STEPS)
    kv_cache, ssm_cache, conv_cache = caches(
        decode_device, block_count, block_slot, kv_all, final_got, here, MOST * here
    )
    return block_out[None], kv_cache[None, None], ssm_cache[None], conv_cache[None]


def solution(mesh):
    return jax.shard_map(
        per_device,
        mesh=mesh,
        in_specs=(
            P("grp", "seq", None),
            P("grp", "seq", None),
            P("grp", "seq", None),
            P("grp", None, None, "seq"),
            P(),
            P(),
            P(),
            P(),
            P(),
            P("grp", "seq", None),
            P(),
            P(),
            P(),
        ),
        out_specs=(
            P("grp", "seq", None),
            P("grp", "seq", None, None, None),
            P("grp", None, None, "seq"),
            P("grp", None, None, "seq"),
        ),
        check_vma=False,
    )
```

```python
import functools

import jax
import jax.numpy as jnp
import numpy as np
from jax import lax
from jax.experimental import pallas as pl
from jax.experimental.pallas import tpu as pltpu
from jax.sharding import PartitionSpec as P

NSTATE = 16
KCONV = 4
BLOCK = 16
MOST = 3
LANES = 128
RIM = 8
STEPS = 8
LOG2E = 1.4426950408889634
LOG2LOG2E = 0.5287663729448977
MSG = 24
VMEM_BYTES = 62 * 1024 * 1024
WIDE_BYTES = 48 * 1024 * 1024
SMALL_BYTES = 16 * 1024 * 1024
F32 = jnp.float32
BF16 = jnp.bfloat16

VM = functools.partial(pl.BlockSpec, memory_space=pltpu.VMEM)
SM = pl.BlockSpec(memory_space=pltpu.SMEM)


def silu_of_half(h):
    return h + h * jnp.tanh(h)


def rate_of(log):
    return jnp.exp2(log * LOG2E + LOG2LOG2E)


def split(v):
    high = v.astype(BF16)
    return high, (v - high.astype(F32)).astype(BF16)


def segment_end(count_ref, length):
    return count_ref[lax.axis_index("grp")] * BLOCK - lax.axis_index("seq") * length


def prepare_kernel(
    width, count_ref, step_ref, sbias_ref, proj_ref, dt_ref, b_ref, c_ref
):
    length, channels = step_ref.shape
    groups = length // NSTATE
    seg_end = segment_end(count_ref, length)

    @pl.when(pl.program_id(0) == 0)
    def _():
        b_rows = proj_ref[0].astype(F32)
        for t in range(length):
            b_ref[t] = jnp.broadcast_to(-b_rows[:, t : t + 1], (NSTATE, LANES))
        wide = NSTATE * NSTATE
        spread = lax.broadcasted_iota(jnp.int32, (NSTATE, wide), 1) % NSTATE
        spread = (spread == lax.broadcasted_iota(jnp.int32, (NSTATE, wide), 0)).astype(BF16)
        tiled = lax.dot_general(
            proj_ref[1], spread, (((0,), (0,)), ((), ())), preferred_element_type=F32
        )
        row = lax.broadcasted_iota(jnp.int32, (length, wide), 0) % NSTATE
        col = lax.broadcasted_iota(jnp.int32, (length, wide), 1) // NSTATE
        c_ref[...] = jnp.where(row == col, tiled, 0.0).astype(BF16).reshape(groups, NSTATE, wide)

    live = lax.broadcasted_iota(jnp.int32, (length, width), 0) < seg_end
    for lane in range(0, channels, width):
        cut = pl.ds(lane, width)
        e = jnp.exp2(step_ref[:, cut].astype(F32) * LOG2E + sbias_ref[:, cut] * LOG2E)
        minus_dt = jnp.where(e < 2e-3, e * (0.5 * e - 1.0), -jnp.log(1.0 + e))
        minus_dt = jnp.where(live, minus_dt, 0.0)
        dt_ref[:, :, cut] = minus_dt.reshape(groups, NSTATE, width)


def prepare(count, step, sbias, proj, steps, width=512):
    length, channels = step.shape
    groups = length // NSTATE
    piece = channels // steps
    blocks = pl.BlockSpec((groups, NSTATE, piece), lambda j: (0, 0, j))
    whole = lambda shape: pl.BlockSpec(shape, lambda j: (0,) * len(shape))
    b_shape = (length, NSTATE, LANES)
    c_shape = (groups, NSTATE, NSTATE * NSTATE)
    return pl.pallas_call(
        functools.partial(prepare_kernel, width),
        grid=(steps,),
        in_specs=[
            SM,
            pl.BlockSpec((length, piece), lambda j: (0, j)),
            pl.BlockSpec((1, piece), lambda j: (0, j)),
            whole(proj.shape),
        ],
        out_specs=[blocks, whole(b_shape), whole(c_shape)],
        out_shape=[
            jax.ShapeDtypeStruct((groups, NSTATE, channels), F32),
            jax.ShapeDtypeStruct(b_shape, F32),
            jax.ShapeDtypeStruct(c_shape, BF16),
        ],
        compiler_params=pltpu.CompilerParams(vmem_limit_bytes=VMEM_BYTES),
        cost_estimate=pl.CostEstimate(
            flops=20 * length * channels,
            bytes_accessed=10 * length * channels,
            transcendentals=2 * length * channels,
        ),
        name="prepare",
    )(count, step, sbias, proj)


def scan_kernel(
    width,
    count_ref,
    x_ref,
    halo_ref,
    dt_ref,
    log_ref,
    cw_ref,
    cbias_ref,
    skip_ref,
    b_ref,
    c_ref,
    shift_ref,
    tri_ref,
    out_ref,
    run_ref,
    msg_ref,
    drive_s,
    rate_s,
):
    length, channels = x_ref.shape
    groups = length // NSTATE
    seg_end = segment_end(count_ref, length)
    held = jnp.logical_and(seg_end >= 1, seg_end <= length).astype(F32)
    tail_at = pl.multiple_of(jnp.clip(seg_end - NSTATE, 0, length - NSTATE), NSTATE)

    base = pl.program_id(0) * channels
    piece = msg_ref.shape[2]

    def tile(l, carry):
        cut = pl.ds(pl.multiple_of(l * width, width), width)
        at = pl.ds(pl.multiple_of(base + l * width, width), width)
        x = x_ref[:, cut]
        moved = jnp.dot(
            shift_ref[...],
            jnp.concatenate([x, halo_ref[:, at]], axis=0),
            preferred_element_type=F32,
        )
        half_w = 0.5 * cw_ref[:, at]
        half = 0.5 * cbias_ref[:, at] + half_w[KCONV - 1 :] * x.astype(F32)
        for k in range(KCONV - 1):
            half = half + half_w[k : k + 1] * moved[k * length : (k + 1) * length]
        driven = silu_of_half(half).reshape(groups, NSTATE, width)
        dt = dt_ref[:, :, cut]
        drive_s[...] = dt * driven
        high, low = split(dt.reshape(length, width))
        run = jnp.dot(
            tri_ref[...], jnp.concatenate([high, low], axis=0), preferred_element_type=F32
        )
        run_ref[:, :, cut] = run.reshape(groups, NSTATE, width)
        out_ref[:, :, cut] = skip_ref[:, at] * driven
        rate_s[...] = rate_of(log_ref[:, at])

        def one_group(i, state):
            rates = rate_s[...]
            mixes = []
            for tt in range(NSTATE):
                dt_now = dt_ref[i, pl.ds(tt, 1), cut]
                drive_now = drive_s[i, pl.ds(tt, 1), :]
                b_now = jnp.concatenate([b_ref[i * NSTATE + tt]] * (width // LANES), axis=1)
                state = jnp.exp2(dt_now * rates) * state + drive_now * b_now
                mixes.append(state.astype(BF16))
            out_ref[i, :, cut] += jnp.dot(
                c_ref[i], jnp.concatenate(mixes, axis=0), preferred_element_type=F32
            )
            return state

        state = lax.fori_loop(0, groups, one_group, jnp.zeros((NSTATE, width), F32), unroll=True)
        s_high, s_low = split(run[length - 1 :])
        tail = x_ref[pl.ds(tail_at, NSTATE), cut].astype(F32) * held
        message = jnp.concatenate(
            [
                state,
                s_high.astype(F32),
                s_low.astype(F32),
                tail[NSTATE - (KCONV - 1) :],
                jnp.zeros((MSG - NSTATE - 2 - (KCONV - 1), width), F32),
            ],
            axis=0,
        )
        inside = pl.ds(pl.multiple_of((l * width) % piece, width), width)
        msg_ref[(l * width) // piece, :, inside] = message.astype(BF16)
        return carry

    lax.fori_loop(0, channels // width, tile, 0, unroll=True)


def local_scan(
    count, x, halo, dt, log, cw, cbias, skip, b_wide, c_diag, pieces, steps, width=512
):
    length, channels = x.shape
    groups = length // NSTATE
    piece = channels // pieces
    block = channels // steps
    rim = halo.shape[0]
    shift = np.zeros(((KCONV - 1) * length, length + rim), np.float32)
    for k in range(KCONV - 1):
        for t in range(length):
            source = t - (KCONV - 1) + k
            shift[k * length + t, source if source >= 0 else length + rim + source] = 1.0
    shift = jnp.asarray(shift, BF16)
    tri = np.tril(np.ones((length, length), np.float32))
    tri = jnp.asarray(np.concatenate([tri, tri], axis=1), BF16)
    per = lambda rows: pl.BlockSpec((rows, block), lambda j: (0, j))
    blocks = pl.BlockSpec((groups, NSTATE, block), lambda j: (0, 0, j))
    whole = lambda a: pl.BlockSpec(a.shape, lambda j: (0,) * a.ndim)
    return pl.pallas_call(
        functools.partial(scan_kernel, width),
        grid=(steps,),
        in_specs=[
            SM,
            per(length),
            whole(halo),
            blocks,
            whole(log),
            whole(cw),
            whole(cbias),
            whole(skip),
            whole(b_wide),
            whole(c_diag),
            whole(shift),
            whole(tri),
        ],
        out_specs=[blocks, blocks, pl.BlockSpec((block // piece, MSG, piece), lambda j: (j, 0, 0))],
        out_shape=[
            jax.ShapeDtypeStruct((groups, NSTATE, channels), F32),
            jax.ShapeDtypeStruct((groups, NSTATE, channels), F32),
            jax.ShapeDtypeStruct((pieces, MSG, piece), BF16),
        ],
        scratch_shapes=[
            pltpu.VMEM((groups, NSTATE, width), F32),
            pltpu.VMEM((NSTATE, width), F32),
        ],
        compiler_params=pltpu.CompilerParams(vmem_limit_bytes=VMEM_BYTES),
        cost_estimate=pl.CostEstimate(
            flops=8 * length * channels * NSTATE,
            bytes_accessed=12 * length * channels,
            transcendentals=length * channels * NSTATE,
        ),
        name="local_scan",
    )(count, x, halo, dt, log, cw, cbias, skip, b_wide, c_diag, shift, tri)


def chain_kernel(dest_ref, got_ref, log_ref, start_ref, final_ref):
    pieces, _, piece = got_ref.shape
    own = pl.ds(pl.multiple_of(lax.axis_index("seq") * piece, piece), piece)
    rates = rate_of(log_ref[:, own])
    state = jnp.zeros((NSTATE, piece), F32)
    tails = jnp.zeros((MSG - NSTATE, piece), F32)
    for r in range(pieces):
        start_ref[r] = state.astype(BF16)
        got = got_ref[r].astype(F32)
        total = got[NSTATE : NSTATE + 1] + got[NSTATE + 1 : NSTATE + 2]
        state = jnp.exp2(total * rates) * state + got[:NSTATE]
        tails = tails + got[NSTATE:]
    final_ref[...] = jnp.zeros_like(final_ref)
    dest = dest_ref[lax.axis_index("grp")]
    rows = tails[2 : 1 + KCONV]
    packed = [state[:, lane : lane + LANES] for lane in range(0, piece, LANES)]
    packed += [rows[:, lane : lane + LANES] for lane in range(0, piece, LANES)]
    final_ref[dest] = jnp.concatenate(packed, axis=0).astype(BF16)


def chain(decode_device, got, log, groups):
    pieces, _, piece = got.shape
    return pl.pallas_call(
        chain_kernel,
        in_specs=[SM, VM(), VM()],
        out_specs=[VM(), VM()],
        out_shape=[
            jax.ShapeDtypeStruct((pieces, NSTATE, piece), BF16),
            jax.ShapeDtypeStruct((groups, (NSTATE + KCONV - 1) * piece // LANES, LANES), BF16),
        ],
        compiler_params=pltpu.CompilerParams(vmem_limit_bytes=SMALL_BYTES),
        name="chain",
    )(decode_device, got, log)


def finish_kernel(
    width, count_ref, start_ref, out_ref, run_ref, log_ref, gate_ref, c_ref, mixed_ref, rate_s, start_s
):
    length, channels = gate_ref.shape
    groups = length // NSTATE
    seg_end = segment_end(count_ref, length)
    base = pl.program_id(0) * channels
    piece = start_ref.shape[2]

    def tile(l, carry):
        cut = pl.ds(pl.multiple_of(l * width, width), width)
        at = pl.ds(pl.multiple_of(base + l * width, width), width)
        inside = pl.ds(pl.multiple_of((l * width) % piece, width), width)
        rate_s[...] = rate_of(log_ref[:, at]).astype(BF16)
        start_s[...] = start_ref[(l * width) // piece, :, inside]

        def one_group(i, carry):
            rates, start = rate_s[...], start_s[...]
            mixes = []
            for tt in range(NSTATE):
                run_now = jnp.broadcast_to(run_ref[i, pl.ds(tt, 1), cut], (NSTATE, width))
                mixes.append(jnp.exp2(run_now.astype(BF16) * rates) * start)
            carried = jnp.dot(
                c_ref[i], jnp.concatenate(mixes, axis=0), preferred_element_type=F32
            )
            rows = pl.ds(pl.multiple_of(i * NSTATE, NSTATE), NSTATE)
            gate = silu_of_half(0.5 * gate_ref[rows, cut].astype(F32))
            mixed = (out_ref[i, :, cut] + carried) * gate
            row = lax.broadcasted_iota(jnp.int32, (NSTATE, width), 0) + i * NSTATE
            mixed_ref[rows, cut] = jnp.where(row < seg_end, mixed, 0.0).astype(BF16)
            return carry

        lax.fori_loop(0, groups, one_group, 0, unroll=True)
        return carry

    lax.fori_loop(0, channels // width, tile, 0)


def finish(count, start, out, run, log, gate, c_diag, steps, width=1024):
    length, channels = gate.shape
    groups = length // NSTATE
    pieces, _, piece = start.shape
    block = channels // steps
    per = lambda rows: pl.BlockSpec((rows, block), lambda j: (0, j))
    blocks = pl.BlockSpec((groups, NSTATE, block), lambda j: (0, 0, j))
    return pl.pallas_call(
        functools.partial(finish_kernel, width),
        grid=(steps,),
        in_specs=[
            SM,
            pl.BlockSpec((block // piece, NSTATE, piece), lambda j: (j, 0, 0)),
            blocks,
            blocks,
            pl.BlockSpec(log.shape, lambda j: (0, 0)),
            per(length),
            pl.BlockSpec(c_diag.shape, lambda j: (0, 0, 0)),
        ],
        out_specs=per(length),
        out_shape=jax.ShapeDtypeStruct((length, channels), BF16),
        scratch_shapes=[pltpu.VMEM((NSTATE, width), BF16), pltpu.VMEM((NSTATE, width), BF16)],
        compiler_params=pltpu.CompilerParams(vmem_limit_bytes=VMEM_BYTES),
        cost_estimate=pl.CostEstimate(
            flops=4 * length * channels * NSTATE,
            bytes_accessed=12 * length * channels,
            transcendentals=length * channels * NSTATE,
        ),
        name="finish",
    )(count, start, out, run, log, gate, c_diag)


def caches_kernel(
    here,
    dest_ref,
    count_ref,
    slot_ref,
    kv_ref,
    got_ref,
    cache_ref,
    state_ref,
    rows_ref,
    kv_sems,
):
    groups = got_ref.shape[0]
    grp_pos = lax.axis_index("grp")
    first = lax.axis_index("seq") * here
    cache_ref[...] = jnp.zeros_like(cache_ref)

    def each_block(act):
        def request(g, carry):
            @pl.when(dest_ref[g] == grp_pos)
            def _():
                def block(j, carry):
                    slot = slot_ref[g, first + j]
                    act(
                        pltpu.make_async_copy(
                            kv_ref.at[g, j], cache_ref.at[slot], kv_sems.at[slot]
                        )
                    )
                    return carry

                lax.fori_loop(0, jnp.clip(count_ref[g] - first, 0, here), block, 0)

            return carry

        lax.fori_loop(0, groups, request, 0)

    each_block(lambda copy: copy.start())
    state_ref[...] = jnp.zeros_like(state_ref)
    rows_ref[...] = jnp.zeros_like(rows_ref)

    def one(g, taken):
        mine = dest_ref[g] == grp_pos

        @pl.when(mine)
        def _():
            got = got_ref[g].astype(F32)
            parts = state_ref.shape[2] // LANES
            tail = got[parts * NSTATE :]
            state = [got[p * NSTATE : (p + 1) * NSTATE] for p in range(parts)]
            rows = [tail[p * (KCONV - 1) : (p + 1) * (KCONV - 1)] for p in range(parts)]
            state_ref[taken] = jnp.concatenate(state, axis=1)
            rows_ref[taken] = jnp.concatenate(rows, axis=1).astype(BF16)

        return taken + mine.astype(jnp.int32)

    lax.fori_loop(0, groups, one, jnp.int32(0))
    each_block(lambda copy: copy.wait())


def caches(decode_device, block_count, block_slot, kv, got, here, capacity, piece):
    width = kv.shape[-1]
    return pl.pallas_call(
        functools.partial(caches_kernel, here),
        in_specs=[
            SM,
            SM,
            SM,
            pl.BlockSpec(memory_space=pl.ANY),
            VM(),
        ],
        out_specs=[VM(), VM(), VM()],
        out_shape=[
            jax.ShapeDtypeStruct((capacity, BLOCK, width), BF16),
            jax.ShapeDtypeStruct((MOST, NSTATE, piece), F32),
            jax.ShapeDtypeStruct((MOST, KCONV - 1, piece), BF16),
        ],
        scratch_shapes=[
            pltpu.SemaphoreType.DMA((capacity,)),
        ],
        compiler_params=pltpu.CompilerParams(vmem_limit_bytes=WIDE_BYTES),
        name="caches",
    )(decode_device, block_count, block_slot, kv, got)


def per_device(
    mamba_input,
    gate_input,
    step_raw,
    scan_proj,
    decay_log,
    step_bias,
    conv_weight,
    conv_bias,
    skip_gain,
    kv_rows,
    decode_device,
    block_count,
    block_slot,
):
    seg_len, channels = mamba_input.shape[1:]
    groups = lax.axis_size("grp")
    pieces = lax.axis_size("seq")
    here = seg_len // BLOCK
    x = mamba_input[0]

    kv_all = lax.all_gather(kv_rows[0].reshape(here, BLOCK, kv_rows.shape[2]), "grp")
    halo = lax.ppermute(x[seg_len - RIM :], "seq", [(s, s + 1) for s in range(pieces - 1)])
    dt, b_wide, c_diag = prepare(block_count, step_raw[0], step_bias[None], scan_proj[0], 2)
    out, run, msg = local_scan(
        block_count,
        x,
        halo,
        dt,
        decay_log,
        conv_weight,
        conv_bias[None],
        skip_gain[None],
        b_wide,
        c_diag,
        pieces,
        STEPS,
    )
    got = lax.all_to_all(msg, "seq", split_axis=0, concat_axis=0, tiled=True)
    starts, final = chain(decode_device, got, decay_log, groups)
    start = lax.all_to_all(starts, "seq", split_axis=0, concat_axis=0, tiled=True)
    final_got = lax.all_to_all(final, "grp", split_axis=0, concat_axis=0, tiled=True)
    block_out = finish(block_count, start, out, run, decay_log, gate_input[0], c_diag, STEPS)
    kv_cache, ssm_cache, conv_cache = caches(
        decode_device, block_count, block_slot, kv_all, final_got, here, MOST * here, channels // pieces
    )
    return block_out[None], kv_cache[None, None], ssm_cache[None], conv_cache[None]


def solution(mesh):
    return jax.shard_map(
        per_device,
        mesh=mesh,
        in_specs=(
            P("grp", "seq", None),
            P("grp", "seq", None),
            P("grp", "seq", None),
            P("grp", None, None, "seq"),
            P(),
            P(),
            P(),
            P(),
            P(),
            P("grp", "seq", None),
            P(),
            P(),
            P(),
        ),
        out_specs=(
            P("grp", "seq", None),
            P("grp", "seq", None, None, None),
            P("grp", None, None, "seq"),
            P("grp", None, None, "seq"),
        ),
        check_vma=False,
    )
```

```python
import functools

import jax
import jax.numpy as jnp
import numpy as np
from jax import lax
from jax.experimental import pallas as pl
from jax.experimental.pallas import tpu as pltpu
from jax.sharding import PartitionSpec as P

NSTATE = 16
KCONV = 4
BLOCK = 16
MOST = 3
LANES = 128
RIM = 8
STEPS = 8
LOG2E = 1.4426950408889634
LOG2LOG2E = 0.5287663729448977
MSG = 24
VMEM_BYTES = 62 * 1024 * 1024
WIDE_BYTES = 48 * 1024 * 1024
SMALL_BYTES = 16 * 1024 * 1024
F32 = jnp.float32
BF16 = jnp.bfloat16

VM = functools.partial(pl.BlockSpec, memory_space=pltpu.VMEM)
SM = pl.BlockSpec(memory_space=pltpu.SMEM)


def silu_of_half(h):
    return h + h * jnp.tanh(h)


def rate_of(log):
    return jnp.exp2(log * LOG2E + LOG2LOG2E)


def split(v):
    high = v.astype(BF16)
    return high, (v - high.astype(F32)).astype(BF16)


def segment_end(count_ref, length):
    return count_ref[lax.axis_index("grp")] * BLOCK - lax.axis_index("seq") * length


def prepare_kernel(
    width, count_ref, step_ref, sbias_ref, proj_ref, dt_ref, b_ref, c_ref
):
    length, channels = step_ref.shape
    groups = length // NSTATE
    seg_end = segment_end(count_ref, length)

    @pl.when(pl.program_id(0) == 0)
    def _():
        b_rows = proj_ref[0].astype(F32)
        for t in range(length):
            b_ref[t] = jnp.broadcast_to(-b_rows[:, t : t + 1], (NSTATE, LANES))
        wide = NSTATE * NSTATE
        spread = lax.broadcasted_iota(jnp.int32, (NSTATE, wide), 1) % NSTATE
        spread = (spread == lax.broadcasted_iota(jnp.int32, (NSTATE, wide), 0)).astype(BF16)
        tiled = lax.dot_general(
            proj_ref[1], spread, (((0,), (0,)), ((), ())), preferred_element_type=F32
        )
        row = lax.broadcasted_iota(jnp.int32, (length, wide), 0) % NSTATE
        col = lax.broadcasted_iota(jnp.int32, (length, wide), 1) // NSTATE
        c_ref[...] = jnp.where(row == col, tiled, 0.0).astype(BF16).reshape(groups, NSTATE, wide)

    live = lax.broadcasted_iota(jnp.int32, (length, width), 0) < seg_end
    for lane in range(0, channels, width):
        cut = pl.ds(lane, width)
        e = jnp.exp2(step_ref[:, cut].astype(F32) * LOG2E + sbias_ref[:, cut] * LOG2E)
        minus_dt = jnp.where(e < 2e-3, e * (0.5 * e - 1.0), -jnp.log(1.0 + e))
        minus_dt = jnp.where(live, minus_dt, 0.0)
        dt_ref[:, :, cut] = minus_dt.reshape(groups, NSTATE, width)


def prepare(count, step, sbias, proj, steps, width=512):
    length, channels = step.shape
    groups = length // NSTATE
    piece = channels // steps
    blocks = pl.BlockSpec((groups, NSTATE, piece), lambda j: (0, 0, j))
    whole = lambda shape: pl.BlockSpec(shape, lambda j: (0,) * len(shape))
    b_shape = (length, NSTATE, LANES)
    c_shape = (groups, NSTATE, NSTATE * NSTATE)
    return pl.pallas_call(
        functools.partial(prepare_kernel, width),
        grid=(steps,),
        in_specs=[
            SM,
            pl.BlockSpec((length, piece), lambda j: (0, j)),
            pl.BlockSpec((1, piece), lambda j: (0, j)),
            whole(proj.shape),
        ],
        out_specs=[blocks, whole(b_shape), whole(c_shape)],
        out_shape=[
            jax.ShapeDtypeStruct((groups, NSTATE, channels), F32),
            jax.ShapeDtypeStruct(b_shape, F32),
            jax.ShapeDtypeStruct(c_shape, BF16),
        ],
        compiler_params=pltpu.CompilerParams(vmem_limit_bytes=VMEM_BYTES),
        cost_estimate=pl.CostEstimate(
            flops=20 * length * channels,
            bytes_accessed=10 * length * channels,
            transcendentals=2 * length * channels,
        ),
        name="prepare",
    )(count, step, sbias, proj)


def scan_kernel(
    width,
    count_ref,
    x_ref,
    halo_ref,
    dt_ref,
    log_ref,
    cw_ref,
    cbias_ref,
    skip_ref,
    b_ref,
    c_ref,
    shift_ref,
    tri_ref,
    out_ref,
    run_ref,
    msg_ref,
    drive_s,
    rate_s,
):
    length, channels = x_ref.shape
    groups = length // NSTATE
    seg_end = segment_end(count_ref, length)
    held = jnp.logical_and(seg_end >= 1, seg_end <= length).astype(F32)
    tail_at = pl.multiple_of(jnp.clip(seg_end - NSTATE, 0, length - NSTATE), NSTATE)

    base = pl.program_id(0) * channels
    piece = msg_ref.shape[2]

    def tile(l, carry):
        cut = pl.ds(pl.multiple_of(l * width, width), width)
        at = pl.ds(pl.multiple_of(base + l * width, width), width)
        x = x_ref[:, cut]
        moved = jnp.dot(
            shift_ref[...],
            jnp.concatenate([x, halo_ref[:, at]], axis=0),
            preferred_element_type=F32,
        )
        half_w = 0.5 * cw_ref[:, at]
        half = 0.5 * cbias_ref[:, at] + half_w[KCONV - 1 :] * x.astype(F32)
        for k in range(KCONV - 1):
            half = half + half_w[k : k + 1] * moved[k * length : (k + 1) * length]
        driven = silu_of_half(half).reshape(groups, NSTATE, width)
        dt = dt_ref[:, :, cut]
        drive_s[...] = dt * driven
        high, low = split(dt.reshape(length, width))
        run = jnp.dot(
            tri_ref[...], jnp.concatenate([high, low], axis=0), preferred_element_type=F32
        )
        run_ref[:, :, cut] = run.reshape(groups, NSTATE, width)
        out_ref[:, :, cut] = skip_ref[:, at] * driven
        rate_s[...] = rate_of(log_ref[:, at])

        def one_group(i, state):
            rates = rate_s[...]
            mixes = []
            for tt in range(NSTATE):
                dt_now = dt_ref[i, pl.ds(tt, 1), cut]
                drive_now = drive_s[i, pl.ds(tt, 1), :]
                b_now = jnp.concatenate([b_ref[i * NSTATE + tt]] * (width // LANES), axis=1)
                state = jnp.exp2(dt_now * rates) * state + drive_now * b_now
                mixes.append(state.astype(BF16))
            out_ref[i, :, cut] += jnp.dot(
                c_ref[i], jnp.concatenate(mixes, axis=0), preferred_element_type=F32
            )
            return state

        state = lax.fori_loop(0, groups, one_group, jnp.zeros((NSTATE, width), F32), unroll=True)
        s_high, s_low = split(run[length - 1 :])
        tail = x_ref[pl.ds(tail_at, NSTATE), cut].astype(F32) * held
        message = jnp.concatenate(
            [
                state,
                s_high.astype(F32),
                s_low.astype(F32),
                tail[NSTATE - (KCONV - 1) :],
                jnp.zeros((MSG - NSTATE - 2 - (KCONV - 1), width), F32),
            ],
            axis=0,
        )
        inside = pl.ds(pl.multiple_of((l * width) % piece, width), width)
        msg_ref[(l * width) // piece, :, inside] = message.astype(BF16)
        return carry

    lax.fori_loop(0, channels // width, tile, 0, unroll=True)


def local_scan(
    count, x, halo, dt, log, cw, cbias, skip, b_wide, c_diag, pieces, steps, width=512
):
    length, channels = x.shape
    groups = length // NSTATE
    piece = channels // pieces
    block = channels // steps
    rim = halo.shape[0]
    shift = np.zeros(((KCONV - 1) * length, length + rim), np.float32)
    for k in range(KCONV - 1):
        for t in range(length):
            source = t - (KCONV - 1) + k
            shift[k * length + t, source if source >= 0 else length + rim + source] = 1.0
    shift = jnp.asarray(shift, BF16)
    tri = np.tril(np.ones((length, length), np.float32))
    tri = jnp.asarray(np.concatenate([tri, tri], axis=1), BF16)
    per = lambda rows: pl.BlockSpec((rows, block), lambda j: (0, j))
    blocks = pl.BlockSpec((groups, NSTATE, block), lambda j: (0, 0, j))
    whole = lambda a: pl.BlockSpec(a.shape, lambda j: (0,) * a.ndim)
    return pl.pallas_call(
        functools.partial(scan_kernel, width),
        grid=(steps,),
        in_specs=[
            SM,
            per(length),
            whole(halo),
            blocks,
            whole(log),
            whole(cw),
            whole(cbias),
            whole(skip),
            whole(b_wide),
            whole(c_diag),
            whole(shift),
            whole(tri),
        ],
        out_specs=[blocks, blocks, pl.BlockSpec((block // piece, MSG, piece), lambda j: (j, 0, 0))],
        out_shape=[
            jax.ShapeDtypeStruct((groups, NSTATE, channels), F32),
            jax.ShapeDtypeStruct((groups, NSTATE, channels), F32),
            jax.ShapeDtypeStruct((pieces, MSG, piece), BF16),
        ],
        scratch_shapes=[
            pltpu.VMEM((groups, NSTATE, width), F32),
            pltpu.VMEM((NSTATE, width), F32),
        ],
        compiler_params=pltpu.CompilerParams(vmem_limit_bytes=VMEM_BYTES),
        cost_estimate=pl.CostEstimate(
            flops=8 * length * channels * NSTATE,
            bytes_accessed=12 * length * channels,
            transcendentals=length * channels * NSTATE,
        ),
        name="local_scan",
    )(count, x, halo, dt, log, cw, cbias, skip, b_wide, c_diag, shift, tri)


def chain_kernel(dest_ref, got_ref, log_ref, start_ref, final_ref):
    pieces, _, piece = got_ref.shape
    own = pl.ds(pl.multiple_of(lax.axis_index("seq") * piece, piece), piece)
    rates = rate_of(log_ref[:, own])
    state = jnp.zeros((NSTATE, piece), F32)
    tails = jnp.zeros((MSG - NSTATE, piece), F32)
    for r in range(pieces):
        start_ref[r] = state.astype(BF16)
        got = got_ref[r].astype(F32)
        total = got[NSTATE : NSTATE + 1] + got[NSTATE + 1 : NSTATE + 2]
        state = jnp.exp2(total * rates) * state + got[:NSTATE]
        tails = tails + got[NSTATE:]
    final_ref[...] = jnp.zeros_like(final_ref)
    dest = dest_ref[lax.axis_index("grp")]
    rows = tails[2 : 1 + KCONV]
    packed = [state[:, lane : lane + LANES] for lane in range(0, piece, LANES)]
    packed += [rows[:, lane : lane + LANES] for lane in range(0, piece, LANES)]
    final_ref[dest] = jnp.concatenate(packed, axis=0).astype(BF16)


def chain(decode_device, got, log, groups):
    pieces, _, piece = got.shape
    return pl.pallas_call(
        chain_kernel,
        in_specs=[SM, VM(), VM()],
        out_specs=[VM(), VM()],
        out_shape=[
            jax.ShapeDtypeStruct((pieces, NSTATE, piece), BF16),
            jax.ShapeDtypeStruct((groups, (NSTATE + KCONV - 1) * piece // LANES, LANES), BF16),
        ],
        compiler_params=pltpu.CompilerParams(vmem_limit_bytes=SMALL_BYTES),
        name="chain",
    )(decode_device, got, log)


def finish_kernel(
    width, count_ref, start_ref, out_ref, run_ref, log_ref, gate_ref, c_ref, mixed_ref, rate_s, start_s
):
    length, channels = gate_ref.shape
    groups = length // NSTATE
    seg_end = segment_end(count_ref, length)
    base = pl.program_id(0) * channels
    piece = start_ref.shape[2]

    def tile(l, carry):
        cut = pl.ds(pl.multiple_of(l * width, width), width)
        at = pl.ds(pl.multiple_of(base + l * width, width), width)
        inside = pl.ds(pl.multiple_of((l * width) % piece, width), width)
        rate_s[...] = rate_of(log_ref[:, at]).astype(BF16)
        start_s[...] = start_ref[(l * width) // piece, :, inside]

        def one_group(i, carry):
            rates, start = rate_s[...], start_s[...]
            mixes = []
            for tt in range(NSTATE):
                run_now = jnp.broadcast_to(run_ref[i, pl.ds(tt, 1), cut], (NSTATE, width))
                mixes.append(jnp.exp2(run_now.astype(BF16) * rates) * start)
            carried = jnp.dot(
                c_ref[i], jnp.concatenate(mixes, axis=0), preferred_element_type=F32
            )
            rows = pl.ds(pl.multiple_of(i * NSTATE, NSTATE), NSTATE)
            gate = silu_of_half(0.5 * gate_ref[rows, cut].astype(F32))
            mixed = (out_ref[i, :, cut] + carried) * gate
            row = lax.broadcasted_iota(jnp.int32, (NSTATE, width), 0) + i * NSTATE
            mixed_ref[rows, cut] = jnp.where(row < seg_end, mixed, 0.0).astype(BF16)
            return carry

        lax.fori_loop(0, groups, one_group, 0, unroll=True)
        return carry

    lax.fori_loop(0, channels // width, tile, 0)


def finish(count, start, out, run, log, gate, c_diag, steps, width=1024):
    length, channels = gate.shape
    groups = length // NSTATE
    pieces, _, piece = start.shape
    block = channels // steps
    per = lambda rows: pl.BlockSpec((rows, block), lambda j: (0, j))
    blocks = pl.BlockSpec((groups, NSTATE, block), lambda j: (0, 0, j))
    return pl.pallas_call(
        functools.partial(finish_kernel, width),
        grid=(steps,),
        in_specs=[
            SM,
            pl.BlockSpec((block // piece, NSTATE, piece), lambda j: (j, 0, 0)),
            blocks,
            blocks,
            pl.BlockSpec(log.shape, lambda j: (0, 0)),
            per(length),
            pl.BlockSpec(c_diag.shape, lambda j: (0, 0, 0)),
        ],
        out_specs=per(length),
        out_shape=jax.ShapeDtypeStruct((length, channels), BF16),
        scratch_shapes=[pltpu.VMEM((NSTATE, width), BF16), pltpu.VMEM((NSTATE, width), BF16)],
        compiler_params=pltpu.CompilerParams(vmem_limit_bytes=VMEM_BYTES),
        cost_estimate=pl.CostEstimate(
            flops=4 * length * channels * NSTATE,
            bytes_accessed=12 * length * channels,
            transcendentals=length * channels * NSTATE,
        ),
        name="finish",
    )(count, start, out, run, log, gate, c_diag)


def caches_kernel(
    here,
    dest_ref,
    count_ref,
    slot_ref,
    kv_ref,
    got_ref,
    cache_ref,
    state_ref,
    rows_ref,
    kv_sems,
):
    groups = got_ref.shape[0]
    grp_pos = lax.axis_index("grp")
    first = lax.axis_index("seq") * here
    cache_ref[...] = jnp.zeros_like(cache_ref)

    def each_block(act):
        def request(g, carry):
            @pl.when(dest_ref[g] == grp_pos)
            def _():
                def block(j, carry):
                    slot = slot_ref[g, first + j]
                    act(
                        pltpu.make_async_copy(
                            kv_ref.at[g, j], cache_ref.at[slot], kv_sems.at[slot]
                        )
                    )
                    return carry

                lax.fori_loop(0, jnp.clip(count_ref[g] - first, 0, here), block, 0)

            return carry

        lax.fori_loop(0, groups, request, 0, unroll=True)

    each_block(lambda copy: copy.start())
    state_ref[...] = jnp.zeros_like(state_ref)
    rows_ref[...] = jnp.zeros_like(rows_ref)

    def one(g, taken):
        mine = dest_ref[g] == grp_pos

        @pl.when(mine)
        def _():
            got = got_ref[g].astype(F32)
            parts = state_ref.shape[2] // LANES
            tail = got[parts * NSTATE :]
            state = [got[p * NSTATE : (p + 1) * NSTATE] for p in range(parts)]
            rows = [tail[p * (KCONV - 1) : (p + 1) * (KCONV - 1)] for p in range(parts)]
            state_ref[taken] = jnp.concatenate(state, axis=1)
            rows_ref[taken] = jnp.concatenate(rows, axis=1).astype(BF16)

        return taken + mine.astype(jnp.int32)

    lax.fori_loop(0, groups, one, jnp.int32(0), unroll=True)
    each_block(lambda copy: copy.wait())


def caches(decode_device, block_count, block_slot, kv, got, here, capacity, piece):
    width = kv.shape[-1]
    return pl.pallas_call(
        functools.partial(caches_kernel, here),
        in_specs=[
            SM,
            SM,
            SM,
            pl.BlockSpec(memory_space=pl.ANY),
            VM(),
        ],
        out_specs=[VM(), VM(), VM()],
        out_shape=[
            jax.ShapeDtypeStruct((capacity, BLOCK, width), BF16),
            jax.ShapeDtypeStruct((MOST, NSTATE, piece), F32),
            jax.ShapeDtypeStruct((MOST, KCONV - 1, piece), BF16),
        ],
        scratch_shapes=[
            pltpu.SemaphoreType.DMA((capacity,)),
        ],
        compiler_params=pltpu.CompilerParams(vmem_limit_bytes=WIDE_BYTES),
        name="caches",
    )(decode_device, block_count, block_slot, kv, got)


def per_device(
    mamba_input,
    gate_input,
    step_raw,
    scan_proj,
    decay_log,
    step_bias,
    conv_weight,
    conv_bias,
    skip_gain,
    kv_rows,
    decode_device,
    block_count,
    block_slot,
):
    seg_len, channels = mamba_input.shape[1:]
    groups = lax.axis_size("grp")
    pieces = lax.axis_size("seq")
    here = seg_len // BLOCK
    x = mamba_input[0]

    kv_all = lax.all_gather(kv_rows[0].reshape(here, BLOCK, kv_rows.shape[2]), "grp")
    halo = lax.ppermute(x[seg_len - RIM :], "seq", [(s, s + 1) for s in range(pieces - 1)])
    dt, b_wide, c_diag = prepare(block_count, step_raw[0], step_bias[None], scan_proj[0], 2)
    out, run, msg = local_scan(
        block_count,
        x,
        halo,
        dt,
        decay_log,
        conv_weight,
        conv_bias[None],
        skip_gain[None],
        b_wide,
        c_diag,
        pieces,
        STEPS,
    )
    got = lax.all_to_all(msg, "seq", split_axis=0, concat_axis=0, tiled=True)
    starts, final = chain(decode_device, got, decay_log, groups)
    start = lax.all_to_all(starts, "seq", split_axis=0, concat_axis=0, tiled=True)
    final_got = lax.all_to_all(final, "grp", split_axis=0, concat_axis=0, tiled=True)
    block_out = finish(block_count, start, out, run, decay_log, gate_input[0], c_diag, STEPS)
    kv_cache, ssm_cache, conv_cache = caches(
        decode_device, block_count, block_slot, kv_all, final_got, here, MOST * here, channels // pieces
    )
    return block_out[None], kv_cache[None, None], ssm_cache[None], conv_cache[None]


def solution(mesh):
    return jax.shard_map(
        per_device,
        mesh=mesh,
        in_specs=(
            P("grp", "seq", None),
            P("grp", "seq", None),
            P("grp", "seq", None),
            P("grp", None, None, "seq"),
            P(),
            P(),
            P(),
            P(),
            P(),
            P("grp", "seq", None),
            P(),
            P(),
            P(),
        ),
        out_specs=(
            P("grp", "seq", None),
            P("grp", "seq", None, None, None),
            P("grp", None, None, "seq"),
            P("grp", None, None, "seq"),
        ),
        check_vma=False,
    )
```
